512 devices in a mesh: fsdp: 64 (over x, z), basis: 8 (over y, core).
Axes of the slice: x: 4, y: 4, z: 16, core: 2. Of those that a mesh axis runs over, the one named last changes fastest.
Arguments:
- gradient: bfloat16 [8, 576, 18432], P('basis', 'fsdp'), may hold values from -6000 to 6000
- first_moment: bfloat16 [8, 576, 18432], P('basis', 'fsdp'), may hold values from -0.29882812 to 0.29882812
- second_moment: bfloat16 [8, 576, 18432], P('basis', None, 'fsdp'), may hold values from 0.0099487305 to 0.5
- statistic: float32 [8, 576, 576], P('basis', 'fsdp'), may hold values from -1 to 3, as said below
- eigenbasis: float32 [8, 576, 576], P('basis', 'fsdp'), may hold values from -1 to 2, as said below
Outputs:
- update: bfloat16 [8, 576, 18432], P('basis', 'fsdp')
- new_first: bfloat16 [8, 576, 18432], P('basis', 'fsdp')
- new_second: bfloat16 [8, 576, 18432], P('basis', None, 'fsdp')
- new_stat: float32 [8, 576, 576], P('basis', 'fsdp')
- new_basis: float32 [8, 576, 576], P('basis', 'fsdp')
The draws below stay inside these ranges and needn't reach their ends.
Inputs may be any that keep to these rules, and one draw needn't show every extreme that they name: `statistic`: symmetric in each block, positive definite. `eigenbasis`: each block invertible.
All inputs are finite; a program needn't handle non-finite values.
Results may differ from the reference program's by a relative error of at most 0.00055.
The reference program's roundings to bfloat16 on the way (of `rounded_basis` and `direction`) count: a program that leaves them out, or rounds other values in their place, can miss the bound.
Values may be sent and summed in bfloat16 or wider, within the bound.
No kernel may reach another device: no remote copies, remote signals or barrier semaphores. Data moves between devices by JAX's collectives and lax.ppermute only.
A program may use at most 128 MiB of HBM per device.

```python
import math
import jax
import jax.numpy as jnp
from jax import lax

FF = 18432
BK = 576
NBLK = 8


def draw_gradient(key, part):
    key = jax.random.fold_in(key, 11)
    key_base, key_rows, key_cols = jax.random.split(key, 3)
    position = jnp.arange(BK, dtype=jnp.float32) / BK
    rising = (1.0 + 2.0 * position)[None, :, None]
    row_scale = jnp.exp(jax.random.uniform(key_rows, (NBLK, BK, 1), jnp.float32, 0.0, math.log(10.0)))
    col_scale = jnp.exp(jax.random.uniform(key_cols, (NBLK, 1, FF), jnp.float32, 0.0, math.log(10.0)))
    base = jnp.clip(jax.random.normal(key_base, (NBLK, BK, FF), jnp.float32), -5.0, 5.0)
    return (base * row_scale * col_scale * rising).astype(jnp.bfloat16)


def draw_statistic(key, part):
    key = jax.random.fold_in(key, 23)
    key_noise, key_diag = jax.random.split(key, 2)
    noise = jnp.clip(jax.random.normal(key_noise, (NBLK, BK, BK), jnp.float32), -5.0, 5.0) * (0.15 / math.sqrt(BK))
    symmetric = (noise + jnp.swapaxes(noise, 1, 2)) * 0.7071
    diagonal = jnp.exp(jax.random.uniform(key_diag, (NBLK, BK), jnp.float32, math.log(0.5), math.log(2.0)))
    return symmetric + diagonal[:, :, None] * jnp.eye(BK, dtype=jnp.float32)[None]


def draw_eigenbasis(key, part):
    key = jax.random.fold_in(key, 37)
    noise = jnp.clip(jax.random.normal(key, (NBLK, BK, BK), jnp.float32), -5.0, 5.0) * (0.3 / math.sqrt(BK))
    return noise + jnp.eye(BK, dtype=jnp.float32)[None]


def levels(rng, shape, shards, smallest, largest):
    def one(axis_at, shards_of):
        heights = jax.random.uniform(jax.random.fold_in(jax.random.fold_in(rng, 6), axis_at), (shards_of,), jnp.float32, smallest / len(shards), largest / len(shards))
        return jnp.repeat(jnp.exp(heights), shape[axis_at] // shards_of).reshape((-1,) + (1,) * (len(shape) - axis_at - 1))

    loudness = one(*shards[0])
    for cut in shards[1:]:
        loudness = loudness * one(*cut)
    return loudness


def normal_values(key, extent, scale, limit, cuts=(), held_as=jnp.bfloat16):
    values = scale * jax.random.normal(key, extent, jnp.float32)
    if cuts:
        values = values * levels(key, extent, cuts, -0.22, 0.18)
    return jnp.clip(values, -limit, limit).astype(held_as)


def setup_inputs(seed: int = 0) -> dict:
    key_of = jax.random.split(jax.random.key(seed), 6)
    return {
        "gradient": draw_gradient(jax.random.fold_in(key_of[5], 71), 0),
        "first_moment": normal_values(key_of[1], (NBLK, BK, FF), 0.05, 0.29882812, ((0, 8), (1, 64))),
        "second_moment": jnp.clip(jnp.exp(math.log(0.5) - 3.9171631 * jax.random.uniform(key_of[2], (NBLK, BK, FF), jnp.float32) ** levels(key_of[2], (NBLK, BK, FF), ((0, 8), (2, 64)), -0.2, 0.2)), 0.0099487305, 0.5).astype(jnp.bfloat16),
        "statistic": draw_statistic(jax.random.fold_in(key_of[5], 71), 0),
        "eigenbasis": draw_eigenbasis(jax.random.fold_in(key_of[5], 71), 0),
    }


beta_first = 0.9
beta_second = 0.95
clip_rms = 0.5
tiny_eps = 1e-08

def reference(gradient, first_moment, second_moment, statistic, eigenbasis):
    sums = lax.map(lambda block: jnp.sum(jnp.square(block.astype(jnp.float32))), gradient)
    entries = NBLK * BK * FF
    clip_factor = jnp.minimum(1.0, clip_rms / jnp.sqrt(jnp.sum(sums) / entries + 1e-06))

    def one_block(items):
        grad_block, moment_block, second_block, stat_block, basis_block = items
        rounded_basis = basis_block.astype(jnp.bfloat16)
        grad_rot = jnp.dot(rounded_basis.T.astype(jnp.float32), grad_block.astype(jnp.float32), preferred_element_type=jnp.float32)
        moment_rot = jnp.dot(rounded_basis.T.astype(jnp.float32), moment_block.astype(jnp.float32), preferred_element_type=jnp.float32)
        scaled_rot = clip_factor * grad_rot
        rotated_first = beta_first * moment_rot + (1.0 - beta_first) * scaled_rot
        second_full = beta_second * second_block.astype(jnp.float32) + (1.0 - beta_second) * scaled_rot * scaled_rot
        direction = (rotated_first / (jnp.sqrt(second_full) + tiny_eps)).astype(jnp.bfloat16)
        update = jnp.dot(rounded_basis.astype(jnp.float32), direction.astype(jnp.float32), preferred_element_type=jnp.float32).astype(jnp.bfloat16)
        new_first = (beta_first * moment_block.astype(jnp.float32) + (1.0 - beta_first) * clip_factor * grad_block.astype(jnp.float32)).astype(jnp.bfloat16)
        covariance = jnp.dot(grad_block.astype(jnp.float32), grad_block.T.astype(jnp.float32), preferred_element_type=jnp.float32) / FF
        new_stat = beta_second * stat_block + (1.0 - beta_second) * clip_factor * clip_factor * covariance
        refreshed = jnp.dot(new_stat, basis_block, precision=lax.Precision.HIGHEST)
        gram_matrix = jnp.dot(refreshed.T, refreshed, precision=lax.Precision.HIGHEST)
        factor = jnp.linalg.cholesky(gram_matrix)
        new_basis = lax.linalg.triangular_solve(factor, refreshed, left_side=False, lower=True, transpose_a=True)
        return (update, new_first, second_full.astype(jnp.bfloat16), new_stat, new_basis)
    update, new_first, new_second, new_stat, new_basis = lax.map(one_block, (gradient, first_moment, second_moment, statistic, eigenbasis))
    return (update, new_first, new_second, new_stat, new_basis)
```

```python
import functools

import jax
import jax.numpy as jnp
from jax import lax
from jax.experimental import pallas as pl
from jax.experimental.pallas import tpu as pltpu
from jax.sharding import Mesh, PartitionSpec as P

FF = 18432
BK = 576
NX, NZ, NB = 4, 16, 8
ROWS = 9
XROWS = ROWS * NZ
COLS = FF // (NX * NZ)
REST = COLS - 256
XSTEP = COLS * NZ
PIECES = NX * COLS
TILES = PIECES // 128
PACK = 96
WIDE = 640
BTILES = WIDE // 128
BPACK = 48
ENTRIES = NB * BK * FF
HIGH = lax.Precision.HIGHEST

beta_first = 0.9
beta_second = 0.95
clip_rms = 0.5
tiny_eps = 1e-08

F32 = jnp.float32
BF16 = jnp.bfloat16


def vmem(n):
    return [pl.BlockSpec(memory_space=pltpu.VMEM)] * n


def call(body, out_shape, n_in, scratch=(), flops=0, nbytes=1 << 20):
    outs = out_shape if isinstance(out_shape, (tuple, list)) else (out_shape,)
    return pl.pallas_call(
        body,
        out_shape=tuple(outs),
        in_specs=vmem(n_in),
        out_specs=tuple(vmem(len(outs))),
        scratch_shapes=list(scratch),
        compiler_params=pltpu.CompilerParams(vmem_limit_bytes=48 << 20),
        cost_estimate=pl.CostEstimate(
            flops=flops, bytes_accessed=nbytes, transcendentals=0
        ),
    )


def struct(shape, dtype):
    return jax.ShapeDtypeStruct(shape, dtype)


def pack_natural(src, buf, out_ref):
    lane = lax.broadcasted_iota(jnp.int32, (16, 128), 1)
    for z in range(NZ):
        rest = jnp.zeros((16, 128), F32)
        for xp in range(NX):
            start = XSTEP * xp + COLS * z
            base = start // 128 * 128
            off = start - base
            w = src[:, base : base + 384]
            if off:
                w = pltpu.roll(w, 384 - off, 1)
            for t in range(2):
                at = ROWS * (2 * xp + t)
                buf[at : at + ROWS, :] = w[:ROWS, 128 * t : 128 * t + 128]
            r = w[:, 256:384]
            if xp:
                r = pltpu.roll(r, REST * xp, 1)
            rest = jnp.where((lane >= REST * xp) & (lane < REST * (xp + 1)), r, rest)
        buf[8 * ROWS : 9 * ROWS, :] = rest[:ROWS]
        out_ref[z] = buf[...].astype(BF16)


def pack_gradient_body(g_ref, out_ref, sum_ref, src, buf):
    g = g_ref[0].astype(F32)
    src[:ROWS, :] = g
    buf[9 * ROWS :, :] = jnp.zeros((PACK - 9 * ROWS, 128), F32)
    pack_natural(src, buf, out_ref)
    total = jnp.sum(g * g)
    sum_ref[...] = jnp.full(sum_ref.shape, total, F32)


def pack_moment_body(m_ref, out_ref, src, buf):
    src[:ROWS, :] = m_ref[0].astype(F32)
    buf[9 * ROWS :, :] = jnp.zeros((PACK - 9 * ROWS, 128), F32)
    pack_natural(src, buf, out_ref)


def pack_basis_body(b_ref, sums_ref, out_ref, buf):
    buf[...] = jnp.zeros(buf.shape, F32)
    for t in range(4):
        buf[ROWS * t : ROWS * (t + 1), :] = b_ref[0, :, 128 * t : 128 * t + 128]
    buf[4 * ROWS : 5 * ROWS, 0:64] = b_ref[0, :, 512:576]
    total = jnp.sum(sums_ref[:, 0:1, :], axis=0)
    buf[45:46, :] = total
    for z in range(NZ):
        out_ref[z] = buf[...]


def unpack_rows(in_ref, buf, full):
    for z in range(NZ):
        buf[...] = in_ref[z].astype(F32)
        for t in range(TILES):
            full[ROWS * z : ROWS * (z + 1), 128 * t : 128 * t + 128] = buf[
                ROWS * t : ROWS * (t + 1), :
            ]


def unpack_gradient_body(in_ref, out_ref, buf, full):
    unpack_rows(in_ref, buf, full)
    g = full[...].astype(BF16)
    for xp in range(NX):
        out_ref[xp] = g


def unpack_moment_body(in_ref, out_ref, buf, full):
    unpack_rows(in_ref, buf, full)
    lane = lax.broadcasted_iota(jnp.int32, (XROWS, 128), 1)
    for xp in range(NX):
        out_ref[xp, :, 0:256] = full[:, 256 * xp : 256 * xp + 256].astype(BF16)
        r = full[:, 1024:1152]
        if xp:
            r = pltpu.roll(r, 128 - REST * xp, 1)
        out_ref[xp, :, 256:384] = jnp.where(lane < REST, r, 0.0).astype(BF16)


def covariance_body(own_ref, all_ref, out_ref, prod):
    own = own_ref[0]
    every = all_ref[...].reshape(BK, PIECES)
    prod[:, :BK] = lax.dot_general(
        own, every, (((1,), (1,)), ((), ())), preferred_element_type=F32
    )
    prod[:, BK:] = jnp.zeros((XROWS, WIDE - BK), F32)
    for z in range(NZ):
        for t in range(BTILES):
            out_ref[z, ROWS * t : ROWS * (t + 1), :] = prod[
                ROWS * z : ROWS * (z + 1), 128 * t : 128 * t + 128
            ]
        out_ref[z, 45:48, :] = jnp.zeros((3, 128), F32)


def unpack_square(in_ref, full):
    for f in range(NX * NZ):
        for t in range(BTILES):
            full[ROWS * f : ROWS * (f + 1), 128 * t : 128 * t + 128] = in_ref[
                f, ROWS * t : ROWS * (t + 1), :
            ]


def unpack_basis_body(in_ref, full_ref, round_ref, clip_ref):
    unpack_square(in_ref, full_ref)
    round_ref[...] = full_ref[:, :BK].astype(BF16)
    total = jnp.sum(in_ref[:, 45, :], axis=0, keepdims=True)[:, 0:1] / ENTRIES
    factor = jnp.minimum(1.0, clip_rms / jnp.sqrt(total + 1e-06))
    clip_ref[...] = jnp.broadcast_to(factor, clip_ref.shape)


def refresh_body(rs_ref, stat_ref, basis_ref, clip_ref, stat_out, own_out, pack_out, cov, buf):
    clip = clip_ref[0:1, 0:1]
    buf[...] = jnp.sum(rs_ref[...], axis=0)
    cov[...] = jnp.zeros(cov.shape, F32)
    for t in range(BTILES):
        cov[:ROWS, 128 * t : 128 * t + 128] = buf[ROWS * t : ROWS * (t + 1), :]
    share = cov[:, :BK] / FF
    new_stat = (1.0 - beta_second) * clip * clip * share
    new_stat = new_stat[:ROWS] + beta_second * stat_ref[0]
    stat_out[0] = new_stat
    cov[:ROWS, :BK] = new_stat
    refreshed = jnp.dot(
        cov[:, :BK], basis_ref[...], preferred_element_type=F32, precision=HIGH
    )
    own_out[...] = refreshed
    buf[...] = jnp.zeros(buf.shape, F32)
    cov[...] = refreshed
    for t in range(BTILES):
        buf[ROWS * t : ROWS * (t + 1), :] = cov[:ROWS, 128 * t : 128 * t + 128]
    for z in range(NZ):
        pack_out[z] = buf[...]


def rotate_body(x_ref, g_ref, m_ref, basis_ref, second_ref, clip_ref, up_ref, second_out):
    x = x_ref[0]
    clip = clip_ref[0:1, 0:1]
    basis = basis_ref[...]
    main = g_ref[:, :, pl.ds(pl.multiple_of(256 * x, 128), 256)].reshape(BK, 256)
    rest = g_ref[:, :, 1024:1152].reshape(BK, 128).astype(F32)
    rest = pltpu.roll(rest, lax.rem(128 - REST * x, 128), 1).astype(BF16)
    piece = jnp.concatenate([main, rest], axis=1)
    lead = (((0,), (0,)), ((), ()))
    grad_rot = lax.dot_general(piece, basis, lead, preferred_element_type=F32)[:COLS]
    moment = m_ref[...].reshape(BK, 384)
    moment_rot = lax.dot_general(moment, basis, lead, preferred_element_type=F32)[:COLS]
    scaled = clip * grad_rot
    first = beta_first * moment_rot + (1.0 - beta_first) * scaled
    second = beta_second * second_ref[0].astype(F32) + (1.0 - beta_second) * scaled * scaled
    second_out[0] = second.astype(BF16)
    direction = (first / (jnp.sqrt(second) + tiny_eps)).astype(BF16)
    update = lax.dot_general(
        basis, direction, (((1,), (1,)), ((), ())), preferred_element_type=F32
    )
    for xp in range(NX):
        part = update[XROWS * xp : XROWS * (xp + 1)].astype(BF16)
        up_ref[xp, :, 0:COLS] = part
        up_ref[xp, :, COLS:384] = jnp.zeros((XROWS, 384 - COLS), BF16)


def pack_update_body(in_ref, out_ref, full, buf):
    lane = lax.broadcasted_iota(jnp.int32, (XROWS, 128), 1)
    rest = jnp.zeros((XROWS, 128), F32)
    for xp in range(NX):
        full[:, 256 * xp : 256 * xp + 256] = in_ref[xp, :, 0:256].astype(F32)
        r = in_ref[xp, :, 256:384].astype(F32)
        if xp:
            r = pltpu.roll(r, REST * xp, 1)
        rest = jnp.where((lane >= REST * xp) & (lane < REST * (xp + 1)), r, rest)
    full[:, 1024:1152] = rest
    buf[9 * ROWS :, :] = jnp.zeros((PACK - 9 * ROWS, 128), F32)
    for z in range(NZ):
        for t in range(TILES):
            buf[ROWS * t : ROWS * (t + 1), :] = full[
                ROWS * z : ROWS * (z + 1), 128 * t : 128 * t + 128
            ]
        out_ref[z] = buf[...].astype(BF16)


def unpack_update_body(in_ref, out_ref, buf, row, nat):
    lane = lax.broadcasted_iota(jnp.int32, (16, 128), 1)
    for q in range(NZ // 4):
        for s in range(4):
            buf[...] = in_ref[4 * q + s].astype(F32)
            off = REST * s
            for xp in range(NX):
                for t in range(2):
                    at = ROWS * (2 * xp + t)
                    row[:ROWS, 128 * t : 128 * t + 128] = buf[at : at + ROWS, :]
                row[:ROWS, 256:384] = buf[8 * ROWS : 9 * ROWS, :]
                rest = row[:, 256:384]
                if xp:
                    rest = pltpu.roll(rest, 128 - REST * xp, 1)
                w = jnp.concatenate([row[:, 0:256], rest], axis=1)
                if off:
                    w = pltpu.roll(w, off, 1)
                at = XSTEP * xp + 1152 * q + 256 * s
                if off:
                    nat[:, at : at + 128] = jnp.where(
                        lane >= off, w[:, 0:128], nat[:, at : at + 128]
                    )
                else:
                    nat[:, at : at + 128] = w[:, 0:128]
                nat[:, at + 128 : at + 384] = w[:, 128:384]
    out_ref[0] = nat[:ROWS, :].astype(BF16)


def first_body(g_ref, m_ref, clip_ref, out_ref):
    clip = clip_ref[0:1, 0:1]
    out_ref[0] = (
        beta_first * m_ref[0].astype(F32)
        + (1.0 - beta_first) * clip * g_ref[0].astype(F32)
    ).astype(BF16)


def eliminate(d_ref, e_ref):
    sub = lax.broadcasted_iota(jnp.int32, (8, 128), 0)

    def spread(row):
        return jnp.broadcast_to(row, (8, 128))

    for g in range(16):
        at = slice(8 * g, 8 * g + 8)
        v, f = d_ref[at, :], e_ref[at, :]
        cols = [spread(v[:, 8 * g + c : 8 * g + c + 1]) for c in range(8)]
        scale, upper, lower, coef = [], [], [], {}
        for i in range(8):
            rs = lax.rsqrt(spread(cols[i][i : i + 1, :]))
            left = jnp.where(sub > i, cols[i] * rs, 0.0)
            u = spread(v[i : i + 1, :]) * rs
            e = spread(f[i : i + 1, :]) * rs
            v = v - left * u
            f = jnp.where(sub == i, e, f - left * e)
            for c in range(i + 1, 8):
                coef[i, c] = spread(left[c : c + 1, :])
                cols[c] = cols[c] - left * coef[i, c]
            scale.append(rs)
            upper.append(u)
            lower.append(e)
        e_ref[at, :] = f
        for r in range(g + 1, 16):
            to = slice(8 * r, 8 * r + 8)
            w, h = d_ref[to, :], e_ref[to, :]
            cols = [spread(w[:, 8 * g + c : 8 * g + c + 1]) for c in range(8)]
            for i in range(8):
                k = cols[i] * scale[i]
                w = w - k * upper[i]
                h = h - k * lower[i]
                for c in range(i + 1, 8):
                    cols[c] = cols[c] - k * coef[i, c]
            d_ref[to, :] = w
            e_ref[to, :] = h


def factor_body(in_ref, own_ref, out_ref, full, mat, result, diag, inv):
    unpack_square(in_ref, full)
    rows = full[...]
    gram = lax.dot_general(
        rows, rows, (((0,), (0,)), ((), ())), preferred_element_type=F32, precision=HIGH
    )
    r = lax.broadcasted_iota(jnp.int32, (WIDE, WIDE), 0)
    c = lax.broadcasted_iota(jnp.int32, (WIDE, WIDE), 1)
    mat[:WIDE, :] = jnp.where((r == c) & (r >= BK), 1.0, gram)
    mat[WIDE:, :] = own_ref[...]
    eye = (
        lax.broadcasted_iota(jnp.int32, (128, 128), 0)
        == lax.broadcasted_iota(jnp.int32, (128, 128), 1)
    ).astype(F32)
    across = (((1,), (1,)), ((), ()))

    def panel(p, carry):
        here = pl.ds(pl.multiple_of(128 * p, 128), 128)
        diag[...] = mat[here, here]
        inv[...] = eye
        eliminate(diag, inv)
        part = lax.dot_general(
            mat[:, here], inv[...], across, preferred_element_type=F32, precision=HIGH
        )
        result[:, here] = part[WIDE:]
        mat[...] -= lax.dot_general(
            part, part[:WIDE], across, preferred_element_type=F32, precision=HIGH
        )
        return carry

    lax.fori_loop(0, BTILES, panel, 0)
    out_ref[0] = result[:ROWS, :BK]


def local(gradient, first_moment, second_moment, statistic, eigenbasis):
    def a2a(v, axes):
        return lax.all_to_all(v, axes, 0, 0, tiled=True)

    g_packed, sums = call(
        pack_gradient_body,
        [struct((NZ, PACK, 128), BF16), struct((NB, 8, 128), F32)],
        1,
        [pltpu.VMEM((16, FF), F32), pltpu.VMEM((PACK, 128), F32)],
    )(gradient)
    g_mid = a2a(g_packed, "z")
    sums = a2a(sums, ("y", "c"))
    (b_packed,) = call(
        pack_basis_body,
        struct((NZ, BPACK, 128), F32),
        2,
        [pltpu.VMEM((BPACK, 128), F32)],
    )(eigenbasis, sums)
    b_mid = a2a(b_packed, "z")
    b_all = a2a(jnp.broadcast_to(b_mid.reshape(1, NZ * BPACK, 128), (NX, NZ * BPACK, 128)), "x")
    (m_packed,) = call(
        pack_moment_body,
        struct((NZ, PACK, 128), BF16),
        1,
        [pltpu.VMEM((16, FF), F32), pltpu.VMEM((PACK, 128), F32)],
    )(first_moment)
    m_mid = a2a(m_packed, "z")

    (g_own,) = call(
        unpack_gradient_body,
        struct((NX, XROWS, PIECES), BF16),
        1,
        [pltpu.VMEM((PACK, 128), F32), pltpu.VMEM((XROWS, PIECES), F32)],
    )(g_mid)
    g_all = a2a(g_own, "x")
    (share,) = call(
        covariance_body,
        struct((NZ, BPACK, 128), F32),
        2,
        [pltpu.VMEM((XROWS, WIDE), F32)],
        flops=2 * XROWS * BK * PIECES,
    )(g_own, g_all)
    share = a2a(share, "z")

    basis, rounded, clip = call(
        unpack_basis_body,
        [struct((BK, WIDE), F32), struct((BK, BK), BF16), struct((8, 128), F32)],
        1,
    )(b_all.reshape(NX * NZ, BPACK, 128))

    new_stat, own, r_packed = call(
        refresh_body,
        [
            struct((1, ROWS, BK), F32),
            struct((16, WIDE), F32),
            struct((NZ, BPACK, 128), F32),
        ],
        4,
        [pltpu.VMEM((16, WIDE), F32), pltpu.VMEM((BPACK, 128), F32)],
        flops=12 * 16 * BK * WIDE,
    )(share, statistic, basis, clip)
    r_mid = a2a(r_packed, "z")
    r_all = a2a(jnp.broadcast_to(r_mid.reshape(1, NZ * BPACK, 128), (NX, NZ * BPACK, 128)), "x")

    (m_own,) = call(
        unpack_moment_body,
        struct((NX, XROWS, 384), BF16),
        1,
        [pltpu.VMEM((PACK, 128), F32), pltpu.VMEM((XROWS, PIECES), F32)],
    )(m_mid)
    m_all = a2a(m_own, "x")
    x_at = lax.axis_index("x").astype(jnp.int32).reshape(1)
    rotate = pl.pallas_call(
        rotate_body,
        out_shape=(struct((NX, XROWS, 384), BF16), struct((1, COLS, BK), BF16)),
        in_specs=[pl.BlockSpec(memory_space=pltpu.SMEM)] + vmem(5),
        out_specs=tuple(vmem(2)),
        compiler_params=pltpu.CompilerParams(vmem_limit_bytes=48 << 20),
        cost_estimate=pl.CostEstimate(
            flops=6 * BK * BK * 384, bytes_accessed=4 << 20, transcendentals=0
        ),
    )
    up, new_second = rotate(x_at, g_all, m_all, rounded, jnp.swapaxes(second_moment, 1, 2), clip)
    up = a2a(up, "x")
    (up_packed,) = call(
        pack_update_body,
        struct((NZ, PACK, 128), BF16),
        1,
        [pltpu.VMEM((XROWS, PIECES), F32), pltpu.VMEM((PACK, 128), F32)],
    )(up)
    up_packed = a2a(up_packed, "z")
    (update,) = call(
        unpack_update_body,
        struct((1, ROWS, FF), BF16),
        1,
        [pltpu.VMEM((PACK, 128), F32), pltpu.VMEM((16, 384), F32), pltpu.VMEM((16, FF), F32)],
    )(up_packed)
    (new_first,) = call(first_body, struct((1, ROWS, FF), BF16), 3)(gradient, first_moment, clip)

    (new_basis,) = call(
        factor_body,
        struct((1, ROWS, BK), F32),
        2,
        [
            pltpu.VMEM((BK, WIDE), F32),
            pltpu.VMEM((WIDE + 16, WIDE), F32),
            pltpu.VMEM((16, WIDE), F32),
            pltpu.VMEM((128, 128), F32),
            pltpu.VMEM((128, 128), F32),
        ],
        flops=12 * BK * WIDE * WIDE,
    )(r_all.reshape(NX * NZ, BPACK, 128), own)
    return update, new_first, jnp.swapaxes(new_second, 1, 2), new_stat, new_basis


def solution(mesh):
    grid = Mesh(mesh.devices.reshape(NX, NZ, 4, 2), ("x", "z", "y", "c"))
    rows = P(("y", "c"), ("x", "z"), None)
    cols = P(("y", "c"), None, ("x", "z"))
    return jax.shard_map(
        local,
        mesh=grid,
        in_specs=(rows, rows, cols, rows, rows),
        out_specs=(rows, rows, cols, rows, rows),
        check_vma=False,
    )
```

```python
import functools

import jax
import jax.numpy as jnp
from jax import lax
from jax.experimental import pallas as pl
from jax.experimental.pallas import tpu as pltpu
from jax.sharding import Mesh, PartitionSpec as P

FF = 18432
BK = 576
NX, NZ, NB = 4, 16, 8
ROWS = 9
XROWS = ROWS * NZ
COLS = FF // (NX * NZ)
REST = COLS - 256
XSTEP = COLS * NZ
PIECES = NX * COLS
TILES = PIECES // 128
PACK = 88
WIDE = 640
BTILES = WIDE // 128
BPACK = 48
GROWS = XROWS + 16
APACK = 168
SUMS = XROWS
MOMENT = XROWS + 16
XPACK = MOMENT + XROWS // 3
ENTRIES = NB * BK * FF
HIGH = lax.Precision.HIGHEST

beta_first = 0.9
beta_second = 0.95
clip_rms = 0.5
tiny_eps = 1e-08

F32 = jnp.float32
BF16 = jnp.bfloat16


def vmem(n):
    return [pl.BlockSpec(memory_space=pltpu.VMEM)] * n


def call(
    body, out_shape, args, scratch=(), at=None, after=(), far=(), flops=0, nbytes=1 << 20
):
    outs = out_shape if isinstance(out_shape, (tuple, list)) else (out_shape,)
    head = [] if at is None else [at]
    n_head, n_real, n_after = len(head), len(args), len(after) + len(far)

    def run(*refs):
        body(*refs[: n_head + n_real], *refs[n_head + n_real + n_after :])

    return pl.pallas_call(
        run,
        out_shape=tuple(outs),
        in_specs=[pl.BlockSpec(memory_space=pltpu.SMEM)] * n_head
        + vmem(n_real)
        + vmem(len(after))
        + [pl.BlockSpec(memory_space=pl.ANY)] * len(far),
        out_specs=tuple(vmem(len(outs))),
        scratch_shapes=list(scratch),
        compiler_params=pltpu.CompilerParams(vmem_limit_bytes=16 << 20),
        cost_estimate=pl.CostEstimate(
            flops=flops, bytes_accessed=nbytes, transcendentals=0
        ),
    )(*head, *args, *after, *far)


def back(x, d):
    return lax.rem(x + (NX - d), NX)


def struct(shape, dtype):
    return jax.ShapeDtypeStruct(shape, dtype)


def pack_natural(src, put):
    lane = lax.broadcasted_iota(jnp.int32, (16, 128), 1)
    for z in range(NZ):
        rest = jnp.zeros((16, 128), F32)
        for xp in range(NX):
            start = XSTEP * xp + COLS * z
            base = start // 128 * 128
            off = start - base
            w = src[:, base : base + 384]
            if off:
                w = pltpu.roll(w, 384 - off, 1)
            for t in range(2):
                put(z, 2 * xp + t, w[:ROWS, 128 * t : 128 * t + 128])
            r = w[:, 256:384]
            if xp:
                r = pltpu.roll(r, REST * xp, 1)
            rest = jnp.where((lane >= REST * xp) & (lane < REST * (xp + 1)), r, rest)
        put(z, 8, rest[:ROWS])


def split(v):
    high = v.astype(BF16).astype(F32)
    mid = (v - high).astype(BF16).astype(F32)
    return high, mid, v - high - mid


def pack_body(g_ref, m_ref, out_ref, sum_ref, src, buf):
    buf[:, 18 * ROWS :, :] = jnp.zeros((NZ, APACK - 18 * ROWS, 128), F32)

    def put(first):
        def store(z, t, rows):
            at = ROWS * (first + t)
            buf[z, at : at + ROWS, :] = rows

        return store

    g = g_ref[0].astype(F32)
    sum_ref[...] = jnp.full(sum_ref.shape, jnp.sum(g * g), F32)
    src[:ROWS, :] = g
    pack_natural(src, put(0))
    src[:ROWS, :] = m_ref[0].astype(F32)
    pack_natural(src, put(9))
    for z in range(NZ):
        out_ref[z] = buf[z].astype(BF16)


def pack_basis_body(b_ref, out_ref, buf):
    buf[...] = jnp.zeros(buf.shape, F32)
    for t in range(4):
        buf[ROWS * t : ROWS * (t + 1), :] = b_ref[0, :, 128 * t : 128 * t + 128]
    buf[4 * ROWS : 5 * ROWS, 0:64] = b_ref[0, :, 512:576]
    for z in range(NZ):
        out_ref[z] = buf[...]


def unpack_body(x_ref, in_ref, s0, s1, s2, s3, o0, o1, o2, o3, buf, full_g, full_m, parts):
    x = x_ref[0]
    for z in range(NZ):
        buf[...] = in_ref[z].astype(F32)
        for t in range(TILES):
            here = (slice(ROWS * z, ROWS * (z + 1)), slice(128 * t, 128 * t + 128))
            full_g[here] = buf[ROWS * t : ROWS * (t + 1), :]
            full_m[here] = buf[ROWS * (9 + t) : ROWS * (10 + t), :]

    total = (s0[...] + s1[...]) + (s2[...] + s3[...])
    high, mid, low = split(total)
    row = lax.broadcasted_iota(jnp.int32, (8, 128), 0)
    sums = jnp.where(row == 0, high, jnp.where(row == 1, mid, jnp.where(row == 2, low, 0.0)))
    sums = jnp.concatenate([sums, jnp.zeros((8, 128), F32)], axis=0).astype(BF16)
    g = full_g[...].astype(BF16)

    lane = lax.broadcasted_iota(jnp.int32, (XROWS, 128), 1)
    for xp in range(NX):
        to = lax.rem(xp - x + NX, NX)
        parts[to, :, 0:256] = full_m[:, 256 * xp : 256 * xp + 256].astype(BF16)
        r = full_m[:, 1024:1152]
        if xp:
            r = pltpu.roll(r, 128 - REST * xp, 1)
        parts[to, :, 256:384] = jnp.where(lane < REST, r, 0.0).astype(BF16)
    for d, out in enumerate((o0, o1, o2, o3)):
        out[:XROWS] = g
        for t in range(TILES):
            out[SUMS:MOMENT, 128 * t : 128 * t + 128] = sums
        for k in range(3):
            out[MOMENT:, 384 * k : 384 * k + 384] = parts[d, 48 * k : 48 * k + 48, :]


def covariance_body(x_ref, g0, g1, g2, g3, out_ref, piece_ref, moment_ref, every, prod):
    x = x_ref[0]
    for d, g in enumerate((g0, g1, g2, g3)):
        every[back(x, d)] = g[:XROWS]
        for k in range(3):
            moment_ref[back(x, d), 48 * k : 48 * k + 48, :] = g[
                MOMENT:, 384 * k : 384 * k + 384
            ]
    sums = jnp.zeros((1, 128), F32)
    for g in (g0, g1, g2, g3):
        rows = g[SUMS:MOMENT, 0:128].astype(F32)
        sums = sums + ((rows[0:1] + rows[1:2]) + rows[2:3])
    prod[:, :BK] = lax.dot_general(
        g0[:XROWS],
        every[...].reshape(BK, PIECES),
        (((1,), (1,)), ((), ())),
        preferred_element_type=F32,
    )
    prod[:, BK:] = jnp.zeros((XROWS, WIDE - BK), F32)
    for z in range(NZ):
        for t in range(BTILES):
            out_ref[z, ROWS * t : ROWS * (t + 1), :] = prod[
                ROWS * z : ROWS * (z + 1), 128 * t : 128 * t + 128
            ]
        out_ref[z, 45:48, :] = jnp.broadcast_to(sums, (3, 128))
    main = every[:, :, pl.ds(pl.multiple_of(256 * x, 128), 256)].reshape(BK, 256)
    rest = every[:, :, 1024:1152].reshape(BK, 128).astype(F32)
    piece_ref[:, 0:256] = main
    piece_ref[:, 256:384] = pltpu.roll(rest, lax.rem(128 - REST * x, 128), 1).astype(BF16)


def unpack_square(in_ref, full):
    for f in range(in_ref.shape[0]):
        for t in range(BTILES):
            full[ROWS * f : ROWS * (f + 1), 128 * t : 128 * t + 128] = in_ref[
                f, ROWS * t : ROWS * (t + 1), :
            ]


def unpack_basis_body(x_ref, b0, b1, b2, b3, full_ref, round_ref, buf):
    x = x_ref[0]
    for d, b in enumerate((b0, b1, b2, b3)):
        buf[back(x, d)] = b[...]
    for xp in range(NX):
        unpack_square(buf.at[xp], full_ref.at[XROWS * xp : XROWS * (xp + 1)])
    round_ref[...] = full_ref[:, :BK].astype(BF16)


def refresh_body(rs_ref, stat_ref, basis_ref, stat_out, own_out, pack_out, clip_out, cov, buf):
    buf[...] = jnp.sum(rs_ref[...], axis=0)
    clip = jnp.minimum(1.0, clip_rms / jnp.sqrt(buf[45:46, 0:1] / ENTRIES + 1e-06))
    clip_out[...] = jnp.broadcast_to(clip, clip_out.shape)
    cov[...] = jnp.zeros(cov.shape, F32)
    for t in range(BTILES):
        cov[:ROWS, 128 * t : 128 * t + 128] = buf[ROWS * t : ROWS * (t + 1), :]
    share = cov[:, :BK] / FF
    new_stat = (1.0 - beta_second) * clip * clip * share
    new_stat = new_stat[:ROWS] + beta_second * stat_ref[0]
    stat_out[0] = new_stat
    cov[:ROWS, :BK] = new_stat
    refreshed = jnp.dot(
        cov[:, :BK], basis_ref[...], preferred_element_type=F32, precision=HIGH
    )
    own_out[...] = refreshed
    buf[...] = jnp.zeros(buf.shape, F32)
    cov[...] = refreshed
    for t in range(BTILES):
        buf[ROWS * t : ROWS * (t + 1), :] = cov[:ROWS, 128 * t : 128 * t + 128]
    for z in range(NZ):
        pack_out[z] = buf[...]


def rotate_body(
    x_ref, g_ref, m_ref, basis_ref, second_ref, clip_ref, o0, o1, o2, o3, second_out, update
):
    x = x_ref[0]
    clip = clip_ref[0:1, 0:1]
    basis = basis_ref[...]
    lead = (((0,), (0,)), ((), ()))
    grad_rot = lax.dot_general(g_ref[...], basis, lead, preferred_element_type=F32)[:COLS]
    moment_rot = lax.dot_general(
        m_ref[...].reshape(BK, 384), basis, lead, preferred_element_type=F32
    )[:COLS]
    scaled = clip * grad_rot
    first = beta_first * moment_rot + (1.0 - beta_first) * scaled
    second = beta_second * second_ref[0].astype(F32) + (1.0 - beta_second) * scaled * scaled
    second_out[0] = second.astype(BF16)
    direction = (first / (jnp.sqrt(second) + tiny_eps)).astype(BF16)
    product = lax.dot_general(
        basis, direction, (((1,), (1,)), ((), ())), preferred_element_type=F32
    )
    for xp in range(NX):
        to = lax.rem(xp - x + NX, NX)
        update[to, :, 0:COLS] = product[XROWS * xp : XROWS * (xp + 1)].astype(BF16)
        update[to, :, COLS:384] = jnp.zeros((XROWS, 384 - COLS), BF16)
    for d, out in enumerate((o0, o1, o2, o3)):
        out[...] = update[d]


def pack_update_body(x_ref, u0, u1, u2, u3, out_ref, parts, full, buf):
    x = x_ref[0]
    for d, u in enumerate((u0, u1, u2, u3)):
        parts[back(x, d)] = u[...]
    lane = lax.broadcasted_iota(jnp.int32, (XROWS, 128), 1)
    rest = jnp.zeros((XROWS, 128), F32)
    for xp in range(NX):
        full[:, 256 * xp : 256 * xp + 256] = parts[xp, :, 0:256].astype(F32)
        r = parts[xp, :, 256:384].astype(F32)
        if xp:
            r = pltpu.roll(r, REST * xp, 1)
        rest = jnp.where((lane >= REST * xp) & (lane < REST * (xp + 1)), r, rest)
    full[:, 1024:1152] = rest
    buf[9 * ROWS :, :] = jnp.zeros((PACK - 9 * ROWS, 128), F32)
    for z in range(NZ):
        for t in range(TILES):
            buf[ROWS * t : ROWS * (t + 1), :] = full[
                ROWS * z : ROWS * (z + 1), 128 * t : 128 * t + 128
            ]
        out_ref[z] = buf[...].astype(BF16)


def unpack_update_body(in_ref, out_ref, buf, row, nat):
    lane = lax.broadcasted_iota(jnp.int32, (16, 128), 1)
    for q in range(NZ // 4):
        for s in range(4):
            buf[...] = in_ref[4 * q + s].astype(F32)
            off = REST * s
            for xp in range(NX):
                for t in range(2):
                    at = ROWS * (2 * xp + t)
                    row[:ROWS, 128 * t : 128 * t + 128] = buf[at : at + ROWS, :]
                row[:ROWS, 256:384] = buf[8 * ROWS : 9 * ROWS, :]
                rest = row[:, 256:384]
                if xp:
                    rest = pltpu.roll(rest, 128 - REST * xp, 1)
                w = jnp.concatenate([row[:, 0:256], rest], axis=1)
                if off:
                    w = pltpu.roll(w, off, 1)
                at = XSTEP * xp + 1152 * q + 256 * s
                if off:
                    nat[:, at : at + 128] = jnp.where(
                        lane >= off, w[:, 0:128], nat[:, at : at + 128]
                    )
                else:
                    nat[:, at : at + 128] = w[:, 0:128]
                nat[:, at + 128 : at + 384] = w[:, 128:384]
    out_ref[0] = nat[:ROWS, :].astype(BF16)


def first_body(g_ref, m_ref, clip_ref, out_ref):
    clip = clip_ref[0:1, 0:1]
    out_ref[0] = (
        beta_first * m_ref[0].astype(F32)
        + (1.0 - beta_first) * clip * g_ref[0].astype(F32)
    ).astype(BF16)


def eliminate_rows(m_ref, first, last):
    sub = lax.broadcasted_iota(jnp.int32, (8, 128), 0)
    lane = lax.broadcasted_iota(jnp.int32, (8, 128), 1)

    def spread(row):
        return jnp.broadcast_to(row, (8, 128))

    for g in range(first, last):
        at = slice(8 * g, 8 * g + 8)
        here = (lane >= 8 * g) & (lane < 8 * g + 8)
        v = m_ref[at, :]
        cols = [spread(v[:, 8 * g + c : 8 * g + c + 1]) for c in range(8)]
        v = jnp.where(here, jnp.where(lane == 8 * g + sub, 1.0, 0.0), v)
        scale, pivot, coef = [], [], {}
        for i in range(8):
            rs = lax.rsqrt(spread(cols[i][i : i + 1, :]))
            left = jnp.where(sub > i, cols[i] * rs, 0.0)
            row = spread(v[i : i + 1, :]) * rs
            v = jnp.where(sub == i, row, v - left * row)
            for c in range(i + 1, 8):
                coef[i, c] = spread(left[c : c + 1, :])
                cols[c] = cols[c] - left * coef[i, c]
            scale.append(rs)
            pivot.append(row)
        m_ref[at, :] = v
        for r in range(g + 1, 16):
            to = slice(8 * r, 8 * r + 8)
            w = m_ref[to, :]
            cols = [spread(w[:, 8 * g + c : 8 * g + c + 1]) for c in range(8)]
            w = jnp.where(here, 0.0, w)
            for i in range(8):
                k = cols[i] * scale[i]
                w = w - k * pivot[i]
                for c in range(i + 1, 8):
                    cols[c] = cols[c] - k * coef[i, c]
            m_ref[to, :] = w


def copies_body(in_ref, out_ref):
    for xp in range(NX):
        out_ref[xp] = in_ref[...]


def factor_body(r_ref, own_ref, out_ref, full, mat, result, diag):
    for xp in range(NX):
        unpack_square(r_ref.at[xp], full.at[XROWS * xp : XROWS * (xp + 1)])
    rows = full[...]
    across = (((1,), (1,)), ((), ()))

    for c, w in ((0, 256), (256, 256), (512, 128)):
        mat[c:WIDE, c : c + w] = lax.dot_general(
            rows[:, c:],
            rows[:, c : c + w],
            (((0,), (0,)), ((), ())),
            preferred_element_type=F32,
            precision=HIGH,
        )
    r = lax.broadcasted_iota(jnp.int32, (128, 128), 0)
    c = lax.broadcasted_iota(jnp.int32, (128, 128), 1)
    eye, below = r == c, r >= c
    mat[512:WIDE, 512:] = jnp.where(eye & (r >= BK - 512), 1.0, mat[512:WIDE, 512:])
    mat[WIDE:, :] = own_ref[...]

    def panel(p, carry):
        here = pl.ds(pl.multiple_of(128 * p, 128), 128)
        diag[...] = mat[here, here]
        eliminate_rows(diag, 0, 8)

        @pl.when(p < BTILES - 1)
        def _():
            eliminate_rows(diag, 8, 16)

        inv = jnp.where(below, diag[...], 0.0)
        for k in range(BTILES):

            @pl.when(p == k)
            def _(k=k):
                low = 128 * (k + 1)
                part = lax.dot_general(
                    mat[low:, 128 * k : low],
                    inv,
                    across,
                    preferred_element_type=F32,
                    precision=HIGH,
                )
                result[:, 128 * k : low] = part[WIDE - low :]
                for c in range(low, WIDE, 256):
                    w = min(256, WIDE - c)
                    mat[c:, c : c + w] -= lax.dot_general(
                        part[c - low :],
                        part[c - low : c - low + w],
                        across,
                        preferred_element_type=F32,
                        precision=HIGH,
                    )

        return carry

    lax.fori_loop(0, BTILES, panel, 0)
    out_ref[0] = result[:ROWS, :BK]


def local(gradient, first_moment, second_moment, statistic, eigenbasis):
    x = lax.axis_index("x").astype(jnp.int32).reshape(1)

    def swap(v, axis):
        return lax.all_to_all(v, axis, 0, 0, tiled=True)

    def shift(v, axis, d):
        size = lax.axis_size(axis)
        return lax.ppermute(v, axis, [(k, (k + d) % size) for k in range(size)])

    def spread(v, axis="x"):
        return [v] + [shift(v, axis, d) for d in (1, 2, 3)]

    def deal(parts):
        return [parts[0]] + [shift(parts[d], "x", d) for d in (1, 2, 3)]

    natural = pltpu.VMEM((16, FF), F32)
    chunk = pltpu.VMEM((PACK, 128), F32)
    rows = pltpu.VMEM((XROWS, PIECES), F32)
    parts = pltpu.VMEM((NX, XROWS, 384), BF16)

    packed, sums = call(
        pack_body,
        [struct((NZ, APACK, 128), BF16), struct((8, 128), F32)],
        [gradient, first_moment],
        [natural, pltpu.VMEM((NZ, APACK, 128), F32)],
    )
    mid = swap(packed, "z")
    sums = spread(sums + shift(sums, "c", 1), "y")
    (b_packed,) = call(
        pack_basis_body,
        struct((NZ, BPACK, 128), F32),
        [eigenbasis],
        [pltpu.VMEM((BPACK, 128), F32)],
        after=sums[1:],
        far=[mid],
    )
    b_mid = swap(b_packed, "z")
    over_x = call(
        unpack_body,
        [struct((XPACK, PIECES), BF16)] * 4,
        [mid, *sums],
        [pltpu.VMEM((APACK, 128), F32), rows, rows, parts],
        at=x,
    )
    share, piece, moment = call(
        covariance_body,
        [
            struct((NZ, BPACK, 128), F32),
            struct((BK, 384), BF16),
            struct((NX, XROWS, 384), BF16),
        ],
        deal(over_x),
        [pltpu.VMEM((NX, XROWS, PIECES), BF16), pltpu.VMEM((XROWS, WIDE), F32)],
        at=x,
        flops=2 * XROWS * BK * PIECES,
    )
    share = swap(share, "z")
    basis, rounded = call(
        unpack_basis_body,
        [struct((BK, WIDE), F32), struct((BK, BK), BF16)],
        spread(b_mid),
        [pltpu.VMEM((NX, NZ, BPACK, 128), F32)],
        at=x,
    )

    new_stat, own, r_packed, clip = call(
        refresh_body,
        [
            struct((1, ROWS, BK), F32),
            struct((16, WIDE), F32),
            struct((NZ, BPACK, 128), F32),
            struct((8, 128), F32),
        ],
        [share, statistic, basis],
        [pltpu.VMEM((16, WIDE), F32), pltpu.VMEM((BPACK, 128), F32)],
        flops=12 * 16 * BK * WIDE,
    )
    r_mid = swap(r_packed, "z")

    *up_parts, new_second = call(
        rotate_body,
        [struct((XROWS, 384), BF16)] * 4 + [struct((1, COLS, BK), BF16)],
        [piece, moment, rounded, jnp.swapaxes(second_moment, 1, 2), clip],
        [parts],
        at=x,
        flops=6 * BK * BK * 384,
        nbytes=4 << 20,
    )
    up_parts = deal(up_parts)
    (new_first,) = call(
        first_body, struct((1, ROWS, FF), BF16), [gradient, first_moment, clip]
    )
    (r_copies,) = call(
        copies_body, struct((NX, NZ, BPACK, 128), F32), [r_mid], after=up_parts[1:], far=[new_first]
    )
    r_all = swap(r_copies, "x")
    (up_packed,) = call(
        pack_update_body,
        struct((NZ, PACK, 128), BF16),
        up_parts,
        [parts, rows, chunk],
        at=x,
        after=[r_all],
    )
    up_mid = swap(up_packed, "z")

    (new_basis,) = call(
        factor_body,
        struct((1, ROWS, BK), F32),
        [r_all, own],
        [
            pltpu.VMEM((BK, WIDE), F32),
            pltpu.VMEM((WIDE + 16, WIDE), F32),
            pltpu.VMEM((16, WIDE), F32),
            pltpu.VMEM((128, 128), F32),
        ],
        flops=12 * BK * WIDE * WIDE,
    )
    (update,) = call(
        unpack_update_body,
        struct((1, ROWS, FF), BF16),
        [up_mid],
        [chunk, pltpu.VMEM((16, 384), F32), natural],
    )
    return update, new_first, jnp.swapaxes(new_second, 1, 2), new_stat, new_basis


def solution(mesh):
    grid = Mesh(mesh.devices.reshape(NX, NZ, 4, 2), ("x", "z", "y", "c"))
    rows = P(("y", "c"), ("x", "z"), None)
    cols = P(("y", "c"), None, ("x", "z"))
    return jax.shard_map(
        local,
        mesh=grid,
        in_specs=(rows, rows, cols, rows, rows),
        out_specs=(rows, rows, cols, rows, rows),
        check_vma=False,
    )
```

```python
import functools

import jax
import jax.numpy as jnp
from jax import lax
from jax.experimental import pallas as pl
from jax.experimental.pallas import tpu as pltpu
from jax.sharding import Mesh, PartitionSpec as P

FF = 18432
BK = 576
NX, NZ, NB = 4, 16, 8
ROWS = 9
XROWS = ROWS * NZ
COLS = FF // (NX * NZ)
REST = COLS - 256
XSTEP = COLS * NZ
PIECES = NX * COLS
TILES = PIECES // 128
PACK = 88
WIDE = 640
BTILES = WIDE // 128
BPACK = 48
GROWS = XROWS + 16
APACK = 168
SUMS = XROWS
MOMENT = XROWS + 16
XPACK = MOMENT + XROWS // 3
ENTRIES = NB * BK * FF
HIGH = lax.Precision.HIGHEST

beta_first = 0.9
beta_second = 0.95
clip_rms = 0.5
tiny_eps = 1e-08

F32 = jnp.float32
BF16 = jnp.bfloat16


def vmem(n):
    return [pl.BlockSpec(memory_space=pltpu.VMEM)] * n


def call(
    body, out_shape, args, scratch=(), at=None, after=(), far=(), flops=0, nbytes=1 << 20
):
    outs = out_shape if isinstance(out_shape, (tuple, list)) else (out_shape,)
    head = [] if at is None else [at]
    n_head, n_real, n_after = len(head), len(args), len(after) + len(far)

    def run(*refs):
        body(*refs[: n_head + n_real], *refs[n_head + n_real + n_after :])

    return pl.pallas_call(
        run,
        out_shape=tuple(outs),
        in_specs=[pl.BlockSpec(memory_space=pltpu.SMEM)] * n_head
        + vmem(n_real)
        + vmem(len(after))
        + [pl.BlockSpec(memory_space=pltpu.HBM)] * len(far),
        out_specs=tuple(vmem(len(outs))),
        scratch_shapes=list(scratch),
        compiler_params=pltpu.CompilerParams(vmem_limit_bytes=16 << 20),
        cost_estimate=pl.CostEstimate(
            flops=flops, bytes_accessed=nbytes, transcendentals=0
        ),
    )(*head, *args, *after, *far)


ORDER = (0, 2, 1, 3)


def back(x, d):
    return lax.rem(x + (NX - d), NX)


def struct(shape, dtype):
    return jax.ShapeDtypeStruct(shape, dtype)


def pack_natural(src, last, buf, first):
    lane = lax.broadcasted_iota(jnp.int32, (16, 128), 1)
    row = lax.broadcasted_iota(jnp.int32, (16, 128), 0)
    lane8 = lane[:8]
    for s in range(4):
        off = REST * s
        rest = [jnp.zeros((8, 128), F32)] * 4
        for xp in range(NX):
            for j in range(4):
                z = 4 * j + s
                base = XSTEP * xp + COLS * z - off
                k = 4 * xp + j
                last[k : k + 1, :] = src[8:9, base : base + 384]
                w = src[:8, base : base + 384]
                if off:
                    w = pltpu.roll(w, 384 - off, 1)
                for t in range(2):
                    at = first + ROWS * (2 * xp + t)
                    buf[z, at : at + 8, :] = w[:, 128 * t : 128 * t + 128]
                r = w[:, 256:384]
                if xp:
                    r = pltpu.roll(r, REST * xp, 1)
                mine = (lane8 >= REST * xp) & (lane8 < REST * (xp + 1))
                rest[j] = jnp.where(mine, r, rest[j])
        w = last[...]
        if off:
            w = pltpu.roll(w, 384 - off, 1)
        r = w[:, 256:384]
        turned = r
        for xp in range(1, NX):
            mine = (row >= 4 * xp) & (row < 4 * xp + 4)
            turned = jnp.where(mine, pltpu.roll(r, REST * xp, 1), turned)
        last[:, 0:256] = w[:, 0:256]
        last[:, 256:384] = turned
        for j in range(4):
            z = 4 * j + s
            end = first + 8 * ROWS
            buf[z, end : end + 8, :] = rest[j]
            for xp in range(NX):
                k = 4 * xp + j
                for t in range(2):
                    at = first + ROWS * (2 * xp + t) + 8
                    buf[z, at : at + 1, :] = last[k : k + 1, 128 * t : 128 * t + 128]
                here = slice(REST * xp, REST * (xp + 1))
                buf[z, end + 8 : end + 9, here] = last[
                    k : k + 1, 256 + REST * xp : 256 + REST * (xp + 1)
                ]


def split(v):
    high = v.astype(BF16).astype(F32)
    mid = (v - high).astype(BF16).astype(F32)
    return high, mid, v - high - mid


def pack_body(g_ref, m_ref, out_ref, sum_ref, src, last, buf):
    buf[:, 18 * ROWS :, :] = jnp.zeros((NZ, APACK - 18 * ROWS, 128), F32)
    g = g_ref[0].astype(F32)
    sum_ref[...] = jnp.full(sum_ref.shape, jnp.sum(g * g), F32)
    src[:ROWS, :] = g
    pack_natural(src, last, buf, 0)
    src[:ROWS, :] = m_ref[0].astype(F32)
    pack_natural(src, last, buf, 9 * ROWS)
    for z in range(NZ):
        out_ref[z] = buf[z].astype(BF16)


def pack_basis_body(b_ref, out_ref, buf):
    buf[...] = jnp.zeros(buf.shape, F32)
    for t in range(4):
        buf[ROWS * t : ROWS * (t + 1), :] = b_ref[0, :, 128 * t : 128 * t + 128]
    buf[4 * ROWS : 5 * ROWS, 0:64] = b_ref[0, :, 512:576]
    for z in range(NZ):
        out_ref[z] = buf[...]


def unpack_body(x_ref, in_ref, s0, s1, s2, s3, o0, o1, o2, o3, buf, full_g, full_m, parts):
    x = x_ref[0]
    for z in range(NZ):
        buf[...] = in_ref[z].astype(F32)
        for t in range(TILES):
            here = (slice(ROWS * z, ROWS * (z + 1)), slice(128 * t, 128 * t + 128))
            full_g[here] = buf[ROWS * t : ROWS * (t + 1), :]
            full_m[here] = buf[ROWS * (9 + t) : ROWS * (10 + t), :]

    total = (s0[...] + s1[...]) + (s2[...] + s3[...])
    high, mid, low = split(total)
    row = lax.broadcasted_iota(jnp.int32, (8, 128), 0)
    sums = jnp.where(row == 0, high, jnp.where(row == 1, mid, jnp.where(row == 2, low, 0.0)))
    sums = jnp.concatenate([sums, jnp.zeros((8, 128), F32)], axis=0).astype(BF16)
    g = full_g[...].astype(BF16)

    lane = lax.broadcasted_iota(jnp.int32, (XROWS, 128), 1)
    for xp in range(NX):
        to = lax.rem(xp - x + NX, NX)
        parts[to, :, 0:256] = full_m[:, 256 * xp : 256 * xp + 256].astype(BF16)
        r = full_m[:, 1024:1152]
        if xp:
            r = pltpu.roll(r, 128 - REST * xp, 1)
        parts[to, :, 256:384] = jnp.where(lane < REST, r, 0.0).astype(BF16)
    for d, out in enumerate((o0, o1, o2, o3)):
        out[:XROWS] = g
        for t in range(TILES):
            out[SUMS:MOMENT, 128 * t : 128 * t + 128] = sums
        for k in range(3):
            out[MOMENT:, 384 * k : 384 * k + 384] = parts[d, 48 * k : 48 * k + 48, :]


def covariance_body(x_ref, g0, g1, g2, g3, out_ref, piece_ref, moment_ref, every, prod):
    x = x_ref[0]
    for d, g in zip(ORDER, (g0, g1, g2, g3)):
        every[back(x, d)] = g[:XROWS]
        for k in range(3):
            moment_ref[back(x, d), 48 * k : 48 * k + 48, :] = g[
                MOMENT:, 384 * k : 384 * k + 384
            ]
    sums = jnp.zeros((1, 128), F32)
    for g in (g0, g1, g2, g3):
        rows = g[SUMS:MOMENT, 0:128].astype(F32)
        sums = sums + ((rows[0:1] + rows[1:2]) + rows[2:3])
    prod[:, :BK] = lax.dot_general(
        g0[:XROWS],
        every[...].reshape(BK, PIECES),
        (((1,), (1,)), ((), ())),
        preferred_element_type=F32,
    )
    prod[:, BK:] = jnp.zeros((XROWS, WIDE - BK), F32)
    for z in range(NZ):
        for t in range(BTILES):
            out_ref[z, ROWS * t : ROWS * (t + 1), :] = prod[
                ROWS * z : ROWS * (z + 1), 128 * t : 128 * t + 128
            ]
        out_ref[z, 45:48, :] = jnp.broadcast_to(sums, (3, 128))
    main = every[:, :, pl.ds(pl.multiple_of(256 * x, 128), 256)].reshape(BK, 256)
    rest = every[:, :, 1024:1152].reshape(BK, 128).astype(F32)
    piece_ref[:, 0:256] = main
    piece_ref[:, 256:384] = pltpu.roll(rest, lax.rem(128 - REST * x, 128), 1).astype(BF16)


def unpack_square(in_ref, full):
    for f in range(in_ref.shape[0]):
        for t in range(BTILES):
            full[ROWS * f : ROWS * (f + 1), 128 * t : 128 * t + 128] = in_ref[
                f, ROWS * t : ROWS * (t + 1), :
            ]


def unpack_basis_body(x_ref, b0, b1, b2, b3, full_ref, round_ref, buf):
    x = x_ref[0]
    for d, b in zip(ORDER, (b0, b1, b2, b3)):
        buf[back(x, d)] = b[...]
    for xp in range(NX):
        unpack_square(buf.at[xp], full_ref.at[XROWS * xp : XROWS * (xp + 1)])
    round_ref[...] = full_ref[:, :BK].astype(BF16)


def refresh_body(rs_ref, stat_ref, basis_ref, stat_out, own_out, pack_out, clip_out, cov, buf):
    buf[...] = jnp.sum(rs_ref[...], axis=0)
    clip = jnp.minimum(1.0, clip_rms / jnp.sqrt(buf[45:46, 0:1] / ENTRIES + 1e-06))
    clip_out[...] = jnp.broadcast_to(clip, clip_out.shape)
    cov[...] = jnp.zeros(cov.shape, F32)
    for t in range(BTILES):
        cov[:ROWS, 128 * t : 128 * t + 128] = buf[ROWS * t : ROWS * (t + 1), :]
    share = cov[:, :BK] / FF
    new_stat = (1.0 - beta_second) * clip * clip * share
    new_stat = new_stat[:ROWS] + beta_second * stat_ref[0]
    stat_out[0] = new_stat
    cov[:ROWS, :BK] = new_stat
    refreshed = jnp.dot(
        cov[:, :BK], basis_ref[...], preferred_element_type=F32, precision=HIGH
    )
    own_out[...] = refreshed
    buf[...] = jnp.zeros(buf.shape, F32)
    cov[...] = refreshed
    for t in range(BTILES):
        buf[ROWS * t : ROWS * (t + 1), :] = cov[:ROWS, 128 * t : 128 * t + 128]
    for z in range(NZ):
        pack_out[z] = buf[...]


def rotate_body(
    x_ref, g_ref, m_ref, basis_ref, second_ref, clip_ref, o0, o1, o2, o3, second_out, update
):
    x = x_ref[0]
    clip = clip_ref[0:1, 0:1]
    basis = basis_ref[...]
    lead = (((0,), (0,)), ((), ()))
    grad_rot = lax.dot_general(g_ref[...], basis, lead, preferred_element_type=F32)[:COLS]
    moment_rot = lax.dot_general(
        m_ref[...].reshape(BK, 384), basis, lead, preferred_element_type=F32
    )[:COLS]
    scaled = clip * grad_rot
    first = beta_first * moment_rot + (1.0 - beta_first) * scaled
    second = beta_second * second_ref[0].astype(F32) + (1.0 - beta_second) * scaled * scaled
    second_out[0] = second.astype(BF16)
    direction = (first / (jnp.sqrt(second) + tiny_eps)).astype(BF16)
    product = lax.dot_general(
        basis, direction, (((1,), (1,)), ((), ())), preferred_element_type=F32
    )
    for xp in range(NX):
        to = lax.rem(xp - x + NX, NX)
        update[to, :, 0:COLS] = product[XROWS * xp : XROWS * (xp + 1)].astype(BF16)
        update[to, :, COLS:384] = jnp.zeros((XROWS, 384 - COLS), BF16)
    for d, out in enumerate((o0, o1, o2, o3)):
        out[...] = update[d]


def pack_update_body(x_ref, u0, u1, u2, u3, out_ref, parts, full, buf):
    x = x_ref[0]
    for d, u in zip(ORDER, (u0, u1, u2, u3)):
        parts[back(x, d)] = u[...]
    lane = lax.broadcasted_iota(jnp.int32, (XROWS, 128), 1)
    rest = jnp.zeros((XROWS, 128), F32)
    for xp in range(NX):
        full[:, 256 * xp : 256 * xp + 256] = parts[xp, :, 0:256].astype(F32)
        r = parts[xp, :, 256:384].astype(F32)
        if xp:
            r = pltpu.roll(r, REST * xp, 1)
        rest = jnp.where((lane >= REST * xp) & (lane < REST * (xp + 1)), r, rest)
    full[:, 1024:1152] = rest
    buf[9 * ROWS :, :] = jnp.zeros((PACK - 9 * ROWS, 128), F32)
    for z in range(NZ):
        for t in range(TILES):
            buf[ROWS * t : ROWS * (t + 1), :] = full[
                ROWS * z : ROWS * (z + 1), 128 * t : 128 * t + 128
            ]
        out_ref[z] = buf[...].astype(BF16)


def unpack_update_body(in_ref, out_ref, buf, row, nat):
    lane = lax.broadcasted_iota(jnp.int32, (16, 128), 1)
    for q in range(NZ // 4):
        for s in range(4):
            buf[...] = in_ref[4 * q + s].astype(F32)
            off = REST * s
            for xp in range(NX):
                for t in range(2):
                    at = ROWS * (2 * xp + t)
                    row[:ROWS, 128 * t : 128 * t + 128] = buf[at : at + ROWS, :]
                row[:ROWS, 256:384] = buf[8 * ROWS : 9 * ROWS, :]
                rest = row[:, 256:384]
                if xp:
                    rest = pltpu.roll(rest, 128 - REST * xp, 1)
                w = jnp.concatenate([row[:, 0:256], rest], axis=1)
                if off:
                    w = pltpu.roll(w, off, 1)
                at = XSTEP * xp + 1152 * q + 256 * s
                if off:
                    nat[:, at : at + 128] = jnp.where(
                        lane >= off, w[:, 0:128], nat[:, at : at + 128]
                    )
                else:
                    nat[:, at : at + 128] = w[:, 0:128]
                nat[:, at + 128 : at + 384] = w[:, 128:384]
    out_ref[0] = nat[:ROWS, :].astype(BF16)


def first_body(g_ref, m_ref, clip_ref, out_ref, done_ref):
    done_ref[...] = clip_ref[...]
    clip = clip_ref[0:1, 0:1]
    out_ref[0] = (
        beta_first * m_ref[0].astype(F32)
        + (1.0 - beta_first) * clip * g_ref[0].astype(F32)
    ).astype(BF16)


def eliminate_rows(m_ref, first, last):
    sub = lax.broadcasted_iota(jnp.int32, (8, 128), 0)
    lane = lax.broadcasted_iota(jnp.int32, (8, 128), 1)

    def spread(row):
        return jnp.broadcast_to(row, (8, 128))

    def columns(rows, g):
        return [spread(rows[:, 8 * g + c : 8 * g + c + 1]) for c in range(8)]

    cols = columns(m_ref[8 * first : 8 * first + 8, :], first)
    for g in range(first, last):
        at = slice(8 * g, 8 * g + 8)
        here = (lane >= 8 * g) & (lane < 8 * g + 8)
        v = jnp.where(here, jnp.where(lane == 8 * g + sub, 1.0, 0.0), m_ref[at, :])
        if g + 1 < 16:
            w = m_ref[8 * g + 8 : 8 * g + 16, :]
            down, ahead = columns(w, g), columns(w, g + 1)
        scale, pivot, coef = [], [], {}
        for i in range(8):
            rs = lax.rsqrt(spread(cols[i][i : i + 1, :]))
            left = jnp.where(sub > i, cols[i] * rs, 0.0)
            for c in range(i + 1, 8):
                coef[i, c] = spread(left[c : c + 1, :])
                cols[c] = cols[c] - left * coef[i, c]
            if g + 1 < 16:
                k = down[i] * rs
                for c in range(i + 1, 8):
                    down[c] = down[c] - k * coef[i, c]
                for c in range(8):
                    ahead[c] = ahead[c] - k * spread(k[c : c + 1, :])
                down[i] = k
            row = spread(v[i : i + 1, :]) * rs
            v = jnp.where(sub == i, row, v - left * row)
            scale.append(rs)
            pivot.append(row)
        m_ref[at, :] = v
        for r in range(g + 1, 16):
            to = slice(8 * r, 8 * r + 8)
            w = m_ref[to, :]
            if r > g + 1:
                part = columns(w, g)
            w = jnp.where(here, 0.0, w)
            for i in range(8):
                if r > g + 1:
                    k = part[i] * scale[i]
                    for c in range(i + 1, 8):
                        part[c] = part[c] - k * coef[i, c]
                else:
                    k = down[i]
                w = w - k * pivot[i]
            m_ref[to, :] = w
        if g + 1 < 16:
            cols = ahead


def copies_body(in_ref, out_ref):
    for xp in range(NX):
        out_ref[xp] = in_ref[...]


def factor_body(r_ref, own_ref, out_ref, full, mat, result, diag):
    for xp in range(NX):
        unpack_square(r_ref.at[xp], full.at[XROWS * xp : XROWS * (xp + 1)])
    rows = full[...]
    across = (((1,), (1,)), ((), ()))

    for c, w in ((0, 256), (256, 256), (512, 128)):
        mat[c:WIDE, c : c + w] = lax.dot_general(
            rows[:, c:],
            rows[:, c : c + w],
            (((0,), (0,)), ((), ())),
            preferred_element_type=F32,
            precision=HIGH,
        )
    r = lax.broadcasted_iota(jnp.int32, (128, 128), 0)
    c = lax.broadcasted_iota(jnp.int32, (128, 128), 1)
    eye, below = r == c, r >= c
    mat[512:WIDE, 512:] = jnp.where(eye & (r >= BK - 512), 1.0, mat[512:WIDE, 512:])
    mat[WIDE:, :] = own_ref[...]

    def panel(p, carry):
        here = pl.ds(pl.multiple_of(128 * p, 128), 128)
        diag[...] = mat[here, here]
        eliminate_rows(diag, 0, 8)

        @pl.when(p < BTILES - 1)
        def _():
            eliminate_rows(diag, 8, 16)

        inv = jnp.where(below, diag[...], 0.0)
        for k in range(BTILES):

            @pl.when(p == k)
            def _(k=k):
                low = 128 * (k + 1)
                part = lax.dot_general(
                    mat[low:, 128 * k : low],
                    inv,
                    across,
                    preferred_element_type=F32,
                    precision=HIGH,
                )
                result[:, 128 * k : low] = part[WIDE - low :]
                for c in range(low, WIDE, 256):
                    w = min(256, WIDE - c)
                    mat[c:, c : c + w] -= lax.dot_general(
                        part[c - low :],
                        part[c - low : c - low + w],
                        across,
                        preferred_element_type=F32,
                        precision=HIGH,
                    )

        return carry

    lax.fori_loop(0, BTILES, panel, 0)
    out_ref[0] = result[:ROWS, :BK]


def local(gradient, first_moment, second_moment, statistic, eigenbasis):
    x = lax.axis_index("x").astype(jnp.int32).reshape(1)

    def swap(v, axis):
        return lax.all_to_all(v, axis, 0, 0, tiled=True)

    def shift(v, axis, d):
        size = lax.axis_size(axis)
        return lax.ppermute(v, axis, [(k, (k + d) % size) for k in range(size)])

    def spread(v, axis="x"):
        return [shift(v, axis, d) if d else v for d in ORDER]

    def deal(parts):
        return [shift(parts[d], "x", d) if d else parts[d] for d in ORDER]

    natural = pltpu.VMEM((16, FF), F32)
    chunk = pltpu.VMEM((PACK, 128), F32)
    rows = pltpu.VMEM((XROWS, PIECES), F32)
    parts = pltpu.VMEM((NX, XROWS, 384), BF16)

    packed, sums = call(
        pack_body,
        [struct((NZ, APACK, 128), BF16), struct((8, 128), F32)],
        [gradient, first_moment],
        [natural, pltpu.VMEM((16, 384), F32), pltpu.VMEM((NZ, APACK, 128), F32)],
    )
    mid = swap(packed, "z")
    sums = spread(sums + shift(sums, "c", 1), "y")
    (b_packed,) = call(
        pack_basis_body,
        struct((NZ, BPACK, 128), F32),
        [eigenbasis],
        [pltpu.VMEM((BPACK, 128), F32)],
        after=sums[1:],
        far=[mid],
    )
    b_mid = swap(b_packed, "z")
    over_x = call(
        unpack_body,
        [struct((XPACK, PIECES), BF16)] * 4,
        [mid, *sums],
        [pltpu.VMEM((APACK, 128), F32), rows, rows, parts],
        at=x,
    )
    share, piece, moment = call(
        covariance_body,
        [
            struct((NZ, BPACK, 128), F32),
            struct((BK, 384), BF16),
            struct((NX, XROWS, 384), BF16),
        ],
        deal(over_x),
        [pltpu.VMEM((NX, XROWS, PIECES), BF16), pltpu.VMEM((XROWS, WIDE), F32)],
        at=x,
        flops=2 * XROWS * BK * PIECES,
    )
    share = swap(share, "z")
    basis, rounded = call(
        unpack_basis_body,
        [struct((BK, WIDE), F32), struct((BK, BK), BF16)],
        spread(b_mid),
        [pltpu.VMEM((NX, NZ, BPACK, 128), F32)],
        at=x,
    )

    new_stat, own, r_packed, clip = call(
        refresh_body,
        [
            struct((1, ROWS, BK), F32),
            struct((16, WIDE), F32),
            struct((NZ, BPACK, 128), F32),
            struct((8, 128), F32),
        ],
        [share, statistic, basis],
        [pltpu.VMEM((16, WIDE), F32), pltpu.VMEM((BPACK, 128), F32)],
        flops=12 * 16 * BK * WIDE,
    )
    r_mid = swap(r_packed, "z")

    *up_parts, new_second = call(
        rotate_body,
        [struct((XROWS, 384), BF16)] * 4 + [struct((1, COLS, BK), BF16)],
        [piece, moment, rounded, jnp.swapaxes(second_moment, 1, 2), clip],
        [parts],
        at=x,
        flops=6 * BK * BK * 384,
        nbytes=4 << 20,
    )
    up_parts = deal(up_parts)
    new_first, first_done = call(
        first_body,
        [struct((1, ROWS, FF), BF16), struct((8, 128), F32)],
        [gradient, first_moment, clip],
    )
    (r_copies,) = call(
        copies_body, struct((NX, NZ, BPACK, 128), F32), [r_mid], after=[*up_parts[1:], first_done]
    )
    r_all = swap(r_copies, "x")
    (up_packed,) = call(
        pack_update_body,
        struct((NZ, PACK, 128), BF16),
        up_parts,
        [parts, rows, chunk],
        at=x,
        after=[r_all],
    )
    up_mid = swap(up_packed, "z")

    (new_basis,) = call(
        factor_body,
        struct((1, ROWS, BK), F32),
        [r_all, own],
        [
            pltpu.VMEM((BK, WIDE), F32),
            pltpu.VMEM((WIDE + 16, WIDE), F32),
            pltpu.VMEM((16, WIDE), F32),
            pltpu.VMEM((128, 128), F32),
        ],
        flops=12 * BK * WIDE * WIDE,
    )
    (update,) = call(
        unpack_update_body,
        struct((1, ROWS, FF), BF16),
        [up_mid],
        [chunk, pltpu.VMEM((16, 384), F32), natural],
    )
    return update, new_first, jnp.swapaxes(new_second, 1, 2), new_stat, new_basis


def solution(mesh):
    grid = Mesh(mesh.devices.reshape(NX, NZ, 4, 2), ("x", "z", "y", "c"))
    rows = P(("y", "c"), ("x", "z"), None)
    cols = P(("y", "c"), None, ("x", "z"))
    return jax.shard_map(
        local,
        mesh=grid,
        in_specs=(rows, rows, cols, rows, rows),
        out_specs=(rows, rows, cols, rows, rows),
        check_vma=False,
    )
```

```python
import functools

import jax
import jax.numpy as jnp
from jax import lax
from jax.experimental import pallas as pl
from jax.experimental.pallas import tpu as pltpu
from jax.sharding import Mesh, PartitionSpec as P

FF = 18432
BK = 576
NX, NZ, NB = 4, 16, 8
ROWS = 9
XROWS = ROWS * NZ
COLS = FF // (NX * NZ)
REST = COLS - 256
XSTEP = COLS * NZ
PIECES = NX * COLS
TILES = PIECES // 128
PACK = 88
WIDE = 640
BTILES = WIDE // 128
BPACK = 48
GROWS = XROWS + 16
APACK = 168
SUMS = XROWS
MOMENT = XROWS + 16
XPACK = MOMENT + XROWS // 3
ENTRIES = NB * BK * FF
HIGH = lax.Precision.HIGHEST

beta_first = 0.9
beta_second = 0.95
clip_rms = 0.5
tiny_eps = 1e-08

F32 = jnp.float32
BF16 = jnp.bfloat16


def vmem(n):
    return [pl.BlockSpec(memory_space=pltpu.VMEM)] * n


def call(
    body, out_shape, args, scratch=(), at=None, after=(), far=(), flops=0, nbytes=1 << 20
):
    outs = out_shape if isinstance(out_shape, (tuple, list)) else (out_shape,)
    head = [] if at is None else [at]
    n_head, n_real, n_after = len(head), len(args), len(after) + len(far)

    def run(*refs):
        body(*refs[: n_head + n_real], *refs[n_head + n_real + n_after :])

    return pl.pallas_call(
        run,
        out_shape=tuple(outs),
        in_specs=[pl.BlockSpec(memory_space=pltpu.SMEM)] * n_head
        + vmem(n_real)
        + vmem(len(after))
        + [pl.BlockSpec(memory_space=pltpu.HBM)] * len(far),
        out_specs=tuple(vmem(len(outs))),
        scratch_shapes=list(scratch),
        compiler_params=pltpu.CompilerParams(vmem_limit_bytes=16 << 20),
        cost_estimate=pl.CostEstimate(
            flops=flops, bytes_accessed=nbytes, transcendentals=0
        ),
    )(*head, *args, *after, *far)


ORDER = (0, 2, 1, 3)


def back(x, d):
    return lax.rem(x + (NX - d), NX)


def struct(shape, dtype):
    return jax.ShapeDtypeStruct(shape, dtype)


def pack_natural(src, last, buf, first):
    lane = lax.broadcasted_iota(jnp.int32, (16, 128), 1)
    row = lax.broadcasted_iota(jnp.int32, (16, 128), 0)
    lane8 = lane[:8]
    for s in range(4):
        off = REST * s
        rest = [jnp.zeros((8, 128), F32)] * 4
        for xp in range(NX):
            for j in range(4):
                z = 4 * j + s
                base = XSTEP * xp + COLS * z - off
                k = 4 * xp + j
                last[k : k + 1, :] = src[8:9, base : base + 384]
                w = src[:8, base : base + 384]
                if off:
                    w = pltpu.roll(w, 384 - off, 1)
                for t in range(2):
                    at = first + ROWS * (2 * xp + t)
                    buf[z, at : at + 8, :] = w[:, 128 * t : 128 * t + 128]
                r = w[:, 256:384]
                if xp:
                    r = pltpu.roll(r, REST * xp, 1)
                mine = (lane8 >= REST * xp) & (lane8 < REST * (xp + 1))
                rest[j] = jnp.where(mine, r, rest[j])
        w = last[...]
        if off:
            w = pltpu.roll(w, 384 - off, 1)
        r = w[:, 256:384]
        turned = r
        for xp in range(1, NX):
            mine = (row >= 4 * xp) & (row < 4 * xp + 4)
            turned = jnp.where(mine, pltpu.roll(r, REST * xp, 1), turned)
        last[:, 0:256] = w[:, 0:256]
        last[:, 256:384] = turned
        for j in range(4):
            z = 4 * j + s
            end = first + 8 * ROWS
            buf[z, end : end + 8, :] = rest[j]
            for xp in range(NX):
                k = 4 * xp + j
                for t in range(2):
                    at = first + ROWS * (2 * xp + t) + 8
                    buf[z, at : at + 1, :] = last[k : k + 1, 128 * t : 128 * t + 128]
                here = slice(REST * xp, REST * (xp + 1))
                buf[z, end + 8 : end + 9, here] = last[
                    k : k + 1, 256 + REST * xp : 256 + REST * (xp + 1)
                ]


def split(v):
    high = v.astype(BF16).astype(F32)
    mid = (v - high).astype(BF16).astype(F32)
    return high, mid, v - high - mid


def pack_body(g_ref, m_ref, out_ref, sum_ref, src, last, buf):
    buf[:, 18 * ROWS :, :] = jnp.zeros((NZ, APACK - 18 * ROWS, 128), F32)
    g = g_ref[0].astype(F32)
    sum_ref[...] = jnp.full(sum_ref.shape, jnp.sum(g * g), F32)
    src[:ROWS, :] = g
    pack_natural(src, last, buf, 0)
    src[:ROWS, :] = m_ref[0].astype(F32)
    pack_natural(src, last, buf, 9 * ROWS)
    for z in range(NZ):
        out_ref[z] = buf[z].astype(BF16)


def pack_basis_body(b_ref, out_ref, buf):
    buf[...] = jnp.zeros(buf.shape, F32)
    for t in range(4):
        buf[ROWS * t : ROWS * (t + 1), :] = b_ref[0, :, 128 * t : 128 * t + 128]
    buf[4 * ROWS : 5 * ROWS, 0:64] = b_ref[0, :, 512:576]
    for z in range(NZ):
        out_ref[z] = buf[...]


def unpack_body(x_ref, in_ref, s0, s1, s2, s3, o0, o1, o2, o3, buf, full_g, full_m, parts):
    x = x_ref[0]
    for z in range(NZ):
        buf[...] = in_ref[z].astype(F32)
        for t in range(TILES):
            here = (slice(ROWS * z, ROWS * (z + 1)), slice(128 * t, 128 * t + 128))
            full_g[here] = buf[ROWS * t : ROWS * (t + 1), :]
            full_m[here] = buf[ROWS * (9 + t) : ROWS * (10 + t), :]

    total = (s0[...] + s1[...]) + (s2[...] + s3[...])
    high, mid, low = split(total)
    row = lax.broadcasted_iota(jnp.int32, (8, 128), 0)
    sums = jnp.where(row == 0, high, jnp.where(row == 1, mid, jnp.where(row == 2, low, 0.0)))
    sums = jnp.concatenate([sums, jnp.zeros((8, 128), F32)], axis=0).astype(BF16)
    g = full_g[...].astype(BF16)

    lane = lax.broadcasted_iota(jnp.int32, (XROWS, 128), 1)
    for xp in range(NX):
        to = lax.rem(xp - x + NX, NX)
        parts[to, :, 0:256] = full_m[:, 256 * xp : 256 * xp + 256].astype(BF16)
        r = full_m[:, 1024:1152]
        if xp:
            r = pltpu.roll(r, 128 - REST * xp, 1)
        parts[to, :, 256:384] = jnp.where(lane < REST, r, 0.0).astype(BF16)
    for d, out in enumerate((o0, o1, o2, o3)):
        out[:XROWS] = g
        for t in range(TILES):
            out[SUMS:MOMENT, 128 * t : 128 * t + 128] = sums
        for k in range(3):
            out[MOMENT:, 384 * k : 384 * k + 384] = parts[d, 48 * k : 48 * k + 48, :]


def covariance_body(x_ref, g0, g1, g2, g3, out_ref, piece_ref, moment_ref, every, prod):
    x = x_ref[0]
    for d, g in zip(ORDER, (g0, g1, g2, g3)):
        every[back(x, d)] = g[:XROWS]
        for k in range(3):
            moment_ref[back(x, d), 48 * k : 48 * k + 48, :] = g[
                MOMENT:, 384 * k : 384 * k + 384
            ]
    sums = jnp.zeros((1, 128), F32)
    for g in (g0, g1, g2, g3):
        rows = g[SUMS:MOMENT, 0:128].astype(F32)
        sums = sums + ((rows[0:1] + rows[1:2]) + rows[2:3])
    prod[:, :BK] = lax.dot_general(
        g0[:XROWS],
        every[...].reshape(BK, PIECES),
        (((1,), (1,)), ((), ())),
        preferred_element_type=F32,
    )
    prod[:, BK:] = jnp.zeros((XROWS, WIDE - BK), F32)
    for z in range(NZ):
        for t in range(BTILES):
            out_ref[z, ROWS * t : ROWS * (t + 1), :] = prod[
                ROWS * z : ROWS * (z + 1), 128 * t : 128 * t + 128
            ]
        out_ref[z, 45:48, :] = jnp.broadcast_to(sums, (3, 128))
    main = every[:, :, pl.ds(pl.multiple_of(256 * x, 128), 256)].reshape(BK, 256)
    rest = every[:, :, 1024:1152].reshape(BK, 128).astype(F32)
    piece_ref[:, 0:256] = main
    piece_ref[:, 256:384] = pltpu.roll(rest, lax.rem(128 - REST * x, 128), 1).astype(BF16)


def unpack_square(in_ref, full):
    for f in range(in_ref.shape[0]):
        for t in range(BTILES):
            full[ROWS * f : ROWS * (f + 1), 128 * t : 128 * t + 128] = in_ref[
                f, ROWS * t : ROWS * (t + 1), :
            ]


def unpack_basis_body(x_ref, b0, b1, b2, b3, full_ref, round_ref, buf):
    x = x_ref[0]
    for d, b in zip(ORDER, (b0, b1, b2, b3)):
        buf[back(x, d)] = b[...]
    for xp in range(NX):
        unpack_square(buf.at[xp], full_ref.at[XROWS * xp : XROWS * (xp + 1)])
    round_ref[...] = full_ref[:, :BK].astype(BF16)


def refresh_body(rs_ref, stat_ref, basis_ref, stat_out, own_out, pack_out, clip_out, cov, buf):
    buf[...] = jnp.sum(rs_ref[...], axis=0)
    clip = jnp.minimum(1.0, clip_rms / jnp.sqrt(buf[45:46, 0:1] / ENTRIES + 1e-06))
    clip_out[...] = jnp.broadcast_to(clip, clip_out.shape)
    cov[...] = jnp.zeros(cov.shape, F32)
    for t in range(BTILES):
        cov[:ROWS, 128 * t : 128 * t + 128] = buf[ROWS * t : ROWS * (t + 1), :]
    share = cov[:, :BK] / FF
    new_stat = (1.0 - beta_second) * clip * clip * share
    new_stat = new_stat[:ROWS] + beta_second * stat_ref[0]
    stat_out[0] = new_stat
    cov[:ROWS, :BK] = new_stat
    refreshed = jnp.dot(
        cov[:, :BK], basis_ref[...], preferred_element_type=F32, precision=HIGH
    )
    own_out[...] = refreshed
    buf[...] = jnp.zeros(buf.shape, F32)
    cov[...] = refreshed
    for t in range(BTILES):
        buf[ROWS * t : ROWS * (t + 1), :] = cov[:ROWS, 128 * t : 128 * t + 128]
    for z in range(NZ):
        pack_out[z] = buf[...]


def rotate_body(
    x_ref, g_ref, m_ref, basis_ref, second_ref, clip_ref, o0, o1, o2, o3, second_out, update
):
    x = x_ref[0]
    clip = clip_ref[0:1, 0:1]
    basis = basis_ref[...]
    lead = (((0,), (0,)), ((), ()))
    grad_rot = lax.dot_general(g_ref[...], basis, lead, preferred_element_type=F32)[:COLS]
    moment_rot = lax.dot_general(
        m_ref[...].reshape(BK, 384), basis, lead, preferred_element_type=F32
    )[:COLS]
    scaled = clip * grad_rot
    first = beta_first * moment_rot + (1.0 - beta_first) * scaled
    second = beta_second * second_ref[0].astype(F32) + (1.0 - beta_second) * scaled * scaled
    second_out[0] = second.astype(BF16)
    direction = (first / (jnp.sqrt(second) + tiny_eps)).astype(BF16)
    product = lax.dot_general(
        basis, direction, (((1,), (1,)), ((), ())), preferred_element_type=F32
    )
    for xp in range(NX):
        to = lax.rem(xp - x + NX, NX)
        update[to, :, 0:COLS] = product[XROWS * xp : XROWS * (xp + 1)].astype(BF16)
        update[to, :, COLS:384] = jnp.zeros((XROWS, 384 - COLS), BF16)
    for d, out in enumerate((o0, o1, o2, o3)):
        out[...] = update[d]


def pack_update_body(x_ref, u0, u1, u2, u3, out_ref, parts, full, buf):
    x = x_ref[0]
    for d, u in zip(ORDER, (u0, u1, u2, u3)):
        parts[back(x, d)] = u[...]
    lane = lax.broadcasted_iota(jnp.int32, (XROWS, 128), 1)
    rest = jnp.zeros((XROWS, 128), F32)
    for xp in range(NX):
        full[:, 256 * xp : 256 * xp + 256] = parts[xp, :, 0:256].astype(F32)
        r = parts[xp, :, 256:384].astype(F32)
        if xp:
            r = pltpu.roll(r, REST * xp, 1)
        rest = jnp.where((lane >= REST * xp) & (lane < REST * (xp + 1)), r, rest)
    full[:, 1024:1152] = rest
    buf[9 * ROWS :, :] = jnp.zeros((PACK - 9 * ROWS, 128), F32)
    for z in range(NZ):
        for t in range(TILES):
            buf[ROWS * t : ROWS * (t + 1), :] = full[
                ROWS * z : ROWS * (z + 1), 128 * t : 128 * t + 128
            ]
        out_ref[z] = buf[...].astype(BF16)


def unpack_update_body(in_ref, out_ref, buf, row, nat):
    lane = lax.broadcasted_iota(jnp.int32, (16, 128), 1)
    for q in range(NZ // 4):
        for s in range(4):
            buf[...] = in_ref[4 * q + s].astype(F32)
            off = REST * s
            for xp in range(NX):
                for t in range(2):
                    at = ROWS * (2 * xp + t)
                    row[:ROWS, 128 * t : 128 * t + 128] = buf[at : at + ROWS, :]
                row[:ROWS, 256:384] = buf[8 * ROWS : 9 * ROWS, :]
                rest = row[:, 256:384]
                if xp:
                    rest = pltpu.roll(rest, 128 - REST * xp, 1)
                w = jnp.concatenate([row[:, 0:256], rest], axis=1)
                if off:
                    w = pltpu.roll(w, off, 1)
                at = XSTEP * xp + 1152 * q + 256 * s
                if off:
                    nat[:, at : at + 128] = jnp.where(
                        lane >= off, w[:, 0:128], nat[:, at : at + 128]
                    )
                else:
                    nat[:, at : at + 128] = w[:, 0:128]
                nat[:, at + 128 : at + 384] = w[:, 128:384]
    out_ref[0] = nat[:ROWS, :].astype(BF16)


def first_body(g_ref, m_ref, clip_ref, out_ref, done_ref):
    done_ref[...] = clip_ref[...]
    clip = clip_ref[0:1, 0:1]
    out_ref[0] = (
        beta_first * m_ref[0].astype(F32)
        + (1.0 - beta_first) * clip * g_ref[0].astype(F32)
    ).astype(BF16)


def eliminate_rows(m_ref, first, last):
    sub = lax.broadcasted_iota(jnp.int32, (8, 128), 0)
    lane = lax.broadcasted_iota(jnp.int32, (8, 128), 1)

    def spread(row):
        return jnp.broadcast_to(row, (8, 128))

    def columns(rows, g):
        return [spread(rows[:, 8 * g + c : 8 * g + c + 1]) for c in range(8)]

    cols = columns(m_ref[8 * first : 8 * first + 8, :], first)
    for g in range(first, last):
        at = slice(8 * g, 8 * g + 8)
        here = (lane >= 8 * g) & (lane < 8 * g + 8)
        v = jnp.where(here, jnp.where(lane == 8 * g + sub, 1.0, 0.0), m_ref[at, :])
        if g + 1 < 16:
            w = m_ref[8 * g + 8 : 8 * g + 16, :]
            down, ahead = columns(w, g), columns(w, g + 1)
        scale, pivot, coef = [], [], {}
        for i in range(8):
            rs = lax.rsqrt(spread(cols[i][i : i + 1, :]))
            left = jnp.where(sub > i, cols[i] * rs, 0.0)
            for c in range(i + 1, 8):
                coef[i, c] = spread(left[c : c + 1, :])
                cols[c] = cols[c] - left * coef[i, c]
            if g + 1 < 16:
                k = down[i] * rs
                for c in range(i + 1, 8):
                    down[c] = down[c] - k * coef[i, c]
                for c in range(8):
                    ahead[c] = ahead[c] - k * spread(k[c : c + 1, :])
                down[i] = k
            row = spread(v[i : i + 1, :]) * rs
            v = jnp.where(sub == i, row, v - left * row)
            scale.append(rs)
            pivot.append(row)
        m_ref[at, :] = v
        for r in range(g + 1, 16):
            to = slice(8 * r, 8 * r + 8)
            w = m_ref[to, :]
            if r > g + 1:
                part = columns(w, g)
            w = jnp.where(here, 0.0, w)
            for i in range(8):
                if r > g + 1:
                    k = part[i] * scale[i]
                    for c in range(i + 1, 8):
                        part[c] = part[c] - k * coef[i, c]
                else:
                    k = down[i]
                w = w - k * pivot[i]
            m_ref[to, :] = w
        if g + 1 < 16:
            cols = ahead


def copy_body(in_ref, out_ref):
    out_ref[...] = in_ref[...]


def factor_body(r0, r1, r2, r3, own_ref, out_ref, full, mat, result, diag):
    for d, r in enumerate((r0, r1, r2, r3)):
        unpack_square(r, full.at[XROWS * d : XROWS * (d + 1)])
    rows = full[...]
    across = (((1,), (1,)), ((), ()))

    for c, w in ((0, 256), (256, 256), (512, 128)):
        mat[c:WIDE, c : c + w] = lax.dot_general(
            rows[:, c:],
            rows[:, c : c + w],
            (((0,), (0,)), ((), ())),
            preferred_element_type=F32,
            precision=HIGH,
        )
    r = lax.broadcasted_iota(jnp.int32, (128, 128), 0)
    c = lax.broadcasted_iota(jnp.int32, (128, 128), 1)
    eye, below = r == c, r >= c
    mat[512:WIDE, 512:] = jnp.where(eye & (r >= BK - 512), 1.0, mat[512:WIDE, 512:])
    mat[WIDE:, :] = own_ref[...]

    def panel(p, carry):
        here = pl.ds(pl.multiple_of(128 * p, 128), 128)
        diag[...] = mat[here, here]
        eliminate_rows(diag, 0, 8)

        @pl.when(p < BTILES - 1)
        def _():
            eliminate_rows(diag, 8, 16)

        inv = jnp.where(below, diag[...], 0.0)
        for k in range(BTILES):

            @pl.when(p == k)
            def _(k=k):
                low = 128 * (k + 1)
                part = lax.dot_general(
                    mat[low:, 128 * k : low],
                    inv,
                    across,
                    preferred_element_type=F32,
                    precision=HIGH,
                )
                result[:, 128 * k : low] = part[WIDE - low :]
                for c in range(low, WIDE, 256):
                    w = min(256, WIDE - c)
                    mat[c:, c : c + w] -= lax.dot_general(
                        part[c - low :],
                        part[c - low : c - low + w],
                        across,
                        preferred_element_type=F32,
                        precision=HIGH,
                    )

        return carry

    lax.fori_loop(0, BTILES, panel, 0)
    out_ref[0] = result[:ROWS, :BK]


def local(gradient, first_moment, second_moment, statistic, eigenbasis):
    x = lax.axis_index("x").astype(jnp.int32).reshape(1)

    def swap(v, axis):
        return lax.all_to_all(v, axis, 0, 0, tiled=True)

    def shift(v, axis, d):
        size = lax.axis_size(axis)
        return lax.ppermute(v, axis, [(k, (k + d) % size) for k in range(size)])

    def spread(v, axis="x"):
        return [shift(v, axis, d) if d else v for d in ORDER]

    def deal(parts):
        return [shift(parts[d], "x", d) if d else parts[d] for d in ORDER]

    natural = pltpu.VMEM((16, FF), F32)
    chunk = pltpu.VMEM((PACK, 128), F32)
    rows = pltpu.VMEM((XROWS, PIECES), F32)
    parts = pltpu.VMEM((NX, XROWS, 384), BF16)

    packed, sums = call(
        pack_body,
        [struct((NZ, APACK, 128), BF16), struct((8, 128), F32)],
        [gradient, first_moment],
        [natural, pltpu.VMEM((16, 384), F32), pltpu.VMEM((NZ, APACK, 128), F32)],
    )
    mid = swap(packed, "z")
    sums = spread(sums + shift(sums, "c", 1), "y")
    (b_packed,) = call(
        pack_basis_body,
        struct((NZ, BPACK, 128), F32),
        [eigenbasis],
        [pltpu.VMEM((BPACK, 128), F32)],
        after=sums[1:],
        far=[mid],
    )
    b_mid = swap(b_packed, "z")
    over_x = call(
        unpack_body,
        [struct((XPACK, PIECES), BF16)] * 4,
        [mid, *sums],
        [pltpu.VMEM((APACK, 128), F32), rows, rows, parts],
        at=x,
    )
    share, piece, moment = call(
        covariance_body,
        [
            struct((NZ, BPACK, 128), F32),
            struct((BK, 384), BF16),
            struct((NX, XROWS, 384), BF16),
        ],
        deal(over_x),
        [pltpu.VMEM((NX, XROWS, PIECES), BF16), pltpu.VMEM((XROWS, WIDE), F32)],
        at=x,
        flops=2 * XROWS * BK * PIECES,
    )
    share = swap(share, "z")
    basis, rounded = call(
        unpack_basis_body,
        [struct((BK, WIDE), F32), struct((BK, BK), BF16)],
        spread(b_mid),
        [pltpu.VMEM((NX, NZ, BPACK, 128), F32)],
        at=x,
    )

    new_stat, own, r_packed, clip = call(
        refresh_body,
        [
            struct((1, ROWS, BK), F32),
            struct((16, WIDE), F32),
            struct((NZ, BPACK, 128), F32),
            struct((8, 128), F32),
        ],
        [share, statistic, basis],
        [pltpu.VMEM((16, WIDE), F32), pltpu.VMEM((BPACK, 128), F32)],
        flops=12 * 16 * BK * WIDE,
    )
    r_mid = swap(r_packed, "z")

    *up_parts, new_second = call(
        rotate_body,
        [struct((XROWS, 384), BF16)] * 4 + [struct((1, COLS, BK), BF16)],
        [piece, moment, rounded, jnp.swapaxes(second_moment, 1, 2), clip],
        [parts],
        at=x,
        flops=6 * BK * BK * 384,
        nbytes=4 << 20,
    )
    up_parts = deal(up_parts)
    new_first, first_done = call(
        first_body,
        [struct((1, ROWS, FF), BF16), struct((8, 128), F32)],
        [gradient, first_moment, clip],
    )
    (r_mid,) = call(
        copy_body,
        struct((NZ, BPACK, 128), F32),
        [r_mid],
        after=[*up_parts[1:], first_done],
    )
    r_parts = spread(r_mid)
    (up_packed,) = call(
        pack_update_body,
        struct((NZ, PACK, 128), BF16),
        up_parts,
        [parts, rows, chunk],
        at=x,
        after=r_parts[1:],
    )
    up_mid = swap(up_packed, "z")

    (new_basis,) = call(
        factor_body,
        struct((1, ROWS, BK), F32),
        [*r_parts, own],
        [
            pltpu.VMEM((BK, WIDE), F32),
            pltpu.VMEM((WIDE + 16, WIDE), F32),
            pltpu.VMEM((16, WIDE), F32),
            pltpu.VMEM((128, 128), F32),
        ],
        flops=12 * BK * WIDE * WIDE,
    )
    (update,) = call(
        unpack_update_body,
        struct((1, ROWS, FF), BF16),
        [up_mid],
        [chunk, pltpu.VMEM((16, 384), F32), natural],
    )
    return update, new_first, jnp.swapaxes(new_second, 1, 2), new_stat, new_basis


def solution(mesh):
    grid = Mesh(mesh.devices.reshape(NX, NZ, 4, 2), ("x", "z", "y", "c"))
    rows = P(("y", "c"), ("x", "z"), None)
    cols = P(("y", "c"), None, ("x", "z"))
    return jax.shard_map(
        local,
        mesh=grid,
        in_specs=(rows, rows, cols, rows, rows),
        out_specs=(rows, rows, cols, rows, rows),
        check_vma=False,
    )
```

```python
import functools

import jax
import jax.numpy as jnp
from jax import lax
from jax.experimental import pallas as pl
from jax.experimental.pallas import tpu as pltpu
from jax.sharding import Mesh, PartitionSpec as P

FF = 18432
BK = 576
NX, NZ, NB = 4, 16, 8
ROWS = 9
XROWS = ROWS * NZ
COLS = FF // (NX * NZ)
REST = COLS - 256
XSTEP = COLS * NZ
PIECES = NX * COLS
TILES = PIECES // 128
PACK = 88
WIDE = 640
BTILES = WIDE // 128
BPACK = 48
GROWS = XROWS + 16
APACK = 168
SUMS = XROWS
MOMENT = XROWS + 16
XPACK = MOMENT + XROWS // 3
ENTRIES = NB * BK * FF
HIGH = lax.Precision.HIGHEST

beta_first = 0.9
beta_second = 0.95
clip_rms = 0.5
tiny_eps = 1e-08

F32 = jnp.float32
BF16 = jnp.bfloat16


def vmem(n):
    return [pl.BlockSpec(memory_space=pltpu.VMEM)] * n


def call(
    body, out_shape, args, scratch=(), at=None, after=(), far=(), flops=0, nbytes=1 << 20
):
    outs = out_shape if isinstance(out_shape, (tuple, list)) else (out_shape,)
    head = [] if at is None else [at]
    n_head, n_real, n_after = len(head), len(args), len(after) + len(far)

    def run(*refs):
        body(*refs[: n_head + n_real], *refs[n_head + n_real + n_after :])

    return pl.pallas_call(
        run,
        out_shape=tuple(outs),
        in_specs=[pl.BlockSpec(memory_space=pltpu.SMEM)] * n_head
        + vmem(n_real)
        + vmem(len(after))
        + [pl.BlockSpec(memory_space=pltpu.HBM)] * len(far),
        out_specs=tuple(vmem(len(outs))),
        scratch_shapes=list(scratch),
        compiler_params=pltpu.CompilerParams(vmem_limit_bytes=16 << 20),
        cost_estimate=pl.CostEstimate(
            flops=flops, bytes_accessed=nbytes, transcendentals=0
        ),
    )(*head, *args, *after, *far)


ORDER = (0, 2, 3, 1)


def back(x, d):
    return lax.rem(x + (NX - d), NX)


def struct(shape, dtype):
    return jax.ShapeDtypeStruct(shape, dtype)


def pack_natural(src, last, buf, first):
    lane = lax.broadcasted_iota(jnp.int32, (16, 128), 1)
    row = lax.broadcasted_iota(jnp.int32, (16, 128), 0)
    lane8 = lane[:8]
    for s in range(4):
        off = REST * s
        rest = [jnp.zeros((8, 128), F32)] * 4
        for xp in range(NX):
            for j in range(4):
                z = 4 * j + s
                base = XSTEP * xp + COLS * z - off
                k = 4 * xp + j
                last[k : k + 1, :] = src[8:9, base : base + 384]
                w = src[:8, base : base + 384]
                if off:
                    w = pltpu.roll(w, 384 - off, 1)
                for t in range(2):
                    at = first + ROWS * (2 * xp + t)
                    buf[z, at : at + 8, :] = w[:, 128 * t : 128 * t + 128]
                r = w[:, 256:384]
                if xp:
                    r = pltpu.roll(r, REST * xp, 1)
                mine = (lane8 >= REST * xp) & (lane8 < REST * (xp + 1))
                rest[j] = jnp.where(mine, r, rest[j])
        w = last[...]
        if off:
            w = pltpu.roll(w, 384 - off, 1)
        r = w[:, 256:384]
        turned = r
        for xp in range(1, NX):
            mine = (row >= 4 * xp) & (row < 4 * xp + 4)
            turned = jnp.where(mine, pltpu.roll(r, REST * xp, 1), turned)
        last[:, 0:256] = w[:, 0:256]
        last[:, 256:384] = turned
        for j in range(4):
            z = 4 * j + s
            end = first + 8 * ROWS
            buf[z, end : end + 8, :] = rest[j]
            for xp in range(NX):
                k = 4 * xp + j
                for t in range(2):
                    at = first + ROWS * (2 * xp + t) + 8
                    buf[z, at : at + 1, :] = last[k : k + 1, 128 * t : 128 * t + 128]
                here = slice(REST * xp, REST * (xp + 1))
                buf[z, end + 8 : end + 9, here] = last[
                    k : k + 1, 256 + REST * xp : 256 + REST * (xp + 1)
                ]


def split(v):
    high = v.astype(BF16).astype(F32)
    mid = (v - high).astype(BF16).astype(F32)
    return high, mid, v - high - mid


def pack_body(g_ref, m_ref, out_ref, sum_ref, src, last, buf):
    buf[:, 18 * ROWS :, :] = jnp.zeros((NZ, APACK - 18 * ROWS, 128), F32)
    g = g_ref[0].astype(F32)
    sum_ref[...] = jnp.full(sum_ref.shape, jnp.sum(g * g), F32)
    src[:ROWS, :] = g
    pack_natural(src, last, buf, 0)
    src[:ROWS, :] = m_ref[0].astype(F32)
    pack_natural(src, last, buf, 9 * ROWS)
    for z in range(NZ):
        out_ref[z] = buf[z].astype(BF16)


def pack_basis_body(b_ref, out_ref, buf):
    buf[...] = jnp.zeros(buf.shape, F32)
    for t in range(4):
        buf[ROWS * t : ROWS * (t + 1), :] = b_ref[0, :, 128 * t : 128 * t + 128]
    buf[4 * ROWS : 5 * ROWS, 0:64] = b_ref[0, :, 512:576]
    for z in range(NZ):
        out_ref[z] = buf[...]


def unpack_body(x_ref, in_ref, s0, s1, s2, s3, o0, o1, o2, o3, buf, full_g, full_m, parts):
    x = x_ref[0]
    for z in range(NZ):
        buf[...] = in_ref[z].astype(F32)
        for t in range(TILES):
            here = (slice(ROWS * z, ROWS * (z + 1)), slice(128 * t, 128 * t + 128))
            full_g[here] = buf[ROWS * t : ROWS * (t + 1), :]
            full_m[here] = buf[ROWS * (9 + t) : ROWS * (10 + t), :]

    total = (s0[...] + s1[...]) + (s2[...] + s3[...])
    high, mid, low = split(total)
    row = lax.broadcasted_iota(jnp.int32, (8, 128), 0)
    sums = jnp.where(row == 0, high, jnp.where(row == 1, mid, jnp.where(row == 2, low, 0.0)))
    sums = jnp.concatenate([sums, jnp.zeros((8, 128), F32)], axis=0).astype(BF16)
    g = full_g[...].astype(BF16)

    lane = lax.broadcasted_iota(jnp.int32, (XROWS, 128), 1)
    for xp in range(NX):
        to = lax.rem(xp - x + NX, NX)
        parts[to, :, 0:256] = full_m[:, 256 * xp : 256 * xp + 256].astype(BF16)
        r = full_m[:, 1024:1152]
        if xp:
            r = pltpu.roll(r, 128 - REST * xp, 1)
        parts[to, :, 256:384] = jnp.where(lane < REST, r, 0.0).astype(BF16)
    for d, out in enumerate((o0, o1, o2, o3)):
        out[:XROWS] = g
        for t in range(TILES):
            out[SUMS:MOMENT, 128 * t : 128 * t + 128] = sums
        for k in range(3):
            out[MOMENT:, 384 * k : 384 * k + 384] = parts[d, 48 * k : 48 * k + 48, :]


def covariance_body(x_ref, g0, g1, g2, g3, out_ref, both_ref, every, prod):
    x = x_ref[0]
    for d, g in zip(ORDER, (g0, g1, g2, g3)):
        every[back(x, d)] = g[:XROWS]
        for k in range(3):
            both_ref[back(x, d), 48 * k : 48 * k + 48, 384:768] = g[
                MOMENT:, 384 * k : 384 * k + 384
            ]
    sums = jnp.zeros((1, 128), F32)
    for g in (g0, g1, g2, g3):
        rows = g[SUMS:MOMENT, 0:128].astype(F32)
        sums = sums + ((rows[0:1] + rows[1:2]) + rows[2:3])
    prod[:, :BK] = lax.dot_general(
        g0[:XROWS],
        every[...].reshape(BK, PIECES),
        (((1,), (1,)), ((), ())),
        preferred_element_type=F32,
    )
    prod[:, BK:] = jnp.zeros((XROWS, WIDE - BK), F32)
    for z in range(NZ):
        for t in range(BTILES):
            out_ref[z, ROWS * t : ROWS * (t + 1), :] = prod[
                ROWS * z : ROWS * (z + 1), 128 * t : 128 * t + 128
            ]
        out_ref[z, 45:48, :] = jnp.broadcast_to(sums, (3, 128))
    both_ref[:, :, 0:256] = every[:, :, pl.ds(pl.multiple_of(256 * x, 128), 256)]
    rest = every[:, :, 1024:1152].reshape(BK, 128).astype(F32)
    rest = pltpu.roll(rest, lax.rem(128 - REST * x, 128), 1).astype(BF16)
    both_ref[:, :, 256:384] = rest.reshape(NX, XROWS, 128)


def unpack_square(in_ref, full):
    for f in range(in_ref.shape[0]):
        for t in range(BTILES):
            full[ROWS * f : ROWS * (f + 1), 128 * t : 128 * t + 128] = in_ref[
                f, ROWS * t : ROWS * (t + 1), :
            ]


def unpack_basis_body(x_ref, b0, b1, b2, b3, full_ref, round_ref, buf):
    x = x_ref[0]
    for d, b in zip(ORDER, (b0, b1, b2, b3)):
        buf[back(x, d)] = b[...]
    for xp in range(NX):
        unpack_square(buf.at[xp], full_ref.at[XROWS * xp : XROWS * (xp + 1)])
    round_ref[...] = full_ref[:, :BK].astype(BF16)


def refresh_body(rs_ref, stat_ref, basis_ref, stat_out, own_out, pack_out, clip_out, cov, buf):
    buf[...] = jnp.sum(rs_ref[...], axis=0)
    clip = jnp.minimum(1.0, clip_rms / jnp.sqrt(buf[45:46, 0:1] / ENTRIES + 1e-06))
    clip_out[...] = jnp.broadcast_to(clip, clip_out.shape)
    cov[...] = jnp.zeros(cov.shape, F32)
    for t in range(BTILES):
        cov[:ROWS, 128 * t : 128 * t + 128] = buf[ROWS * t : ROWS * (t + 1), :]
    share = cov[:, :BK] / FF
    new_stat = (1.0 - beta_second) * clip * clip * share
    new_stat = new_stat[:ROWS] + beta_second * stat_ref[0]
    stat_out[0] = new_stat
    cov[:ROWS, :BK] = new_stat
    refreshed = jnp.dot(
        cov[:, :BK], basis_ref[...], preferred_element_type=F32, precision=HIGH
    )
    own_out[...] = refreshed
    buf[...] = jnp.zeros(buf.shape, F32)
    cov[...] = refreshed
    for t in range(BTILES):
        buf[ROWS * t : ROWS * (t + 1), :] = cov[:ROWS, 128 * t : 128 * t + 128]
    for z in range(NZ):
        pack_out[z] = buf[...]


def rotate_body(
    x_ref, both_ref, basis_ref, second_ref, clip_ref, o0, o1, o2, o3, second_out, update
):
    x = x_ref[0]
    clip = clip_ref[0:1, 0:1]
    basis = basis_ref[...]
    lead = (((0,), (0,)), ((), ()))
    both = both_ref[...].reshape(BK, 768)
    rotated = lax.dot_general(both, basis, lead, preferred_element_type=F32)
    grad_rot, moment_rot = rotated[:COLS], rotated[384 : 384 + COLS]
    scaled = clip * grad_rot
    first = beta_first * moment_rot + (1.0 - beta_first) * scaled
    second = beta_second * second_ref[0].astype(F32) + (1.0 - beta_second) * scaled * scaled
    second_out[0] = second.astype(BF16)
    direction = (first / (jnp.sqrt(second) + tiny_eps)).astype(BF16)
    product = lax.dot_general(
        basis, direction, (((1,), (1,)), ((), ())), preferred_element_type=F32
    )
    for xp in range(NX):
        to = lax.rem(xp - x + NX, NX)
        update[to, :, 0:COLS] = product[XROWS * xp : XROWS * (xp + 1)].astype(BF16)
        update[to, :, COLS:384] = jnp.zeros((XROWS, 384 - COLS), BF16)
    for d, out in enumerate((o0, o1, o2, o3)):
        out[...] = update[d]


def pack_update_body(x_ref, u0, u1, u2, u3, out_ref, parts, full, buf):
    x = x_ref[0]
    for d, u in zip(ORDER, (u0, u1, u2, u3)):
        parts[back(x, d)] = u[...]
    lane = lax.broadcasted_iota(jnp.int32, (XROWS, 128), 1)
    rest = jnp.zeros((XROWS, 128), F32)
    for xp in range(NX):
        full[:, 256 * xp : 256 * xp + 256] = parts[xp, :, 0:256].astype(F32)
        r = parts[xp, :, 256:384].astype(F32)
        if xp:
            r = pltpu.roll(r, REST * xp, 1)
        rest = jnp.where((lane >= REST * xp) & (lane < REST * (xp + 1)), r, rest)
    full[:, 1024:1152] = rest
    buf[9 * ROWS :, :] = jnp.zeros((PACK - 9 * ROWS, 128), F32)
    for z in range(NZ):
        for t in range(TILES):
            buf[ROWS * t : ROWS * (t + 1), :] = full[
                ROWS * z : ROWS * (z + 1), 128 * t : 128 * t + 128
            ]
        out_ref[z] = buf[...].astype(BF16)


def unpack_update_body(in_ref, out_ref, buf, row, nat):
    lane = lax.broadcasted_iota(jnp.int32, (16, 128), 1)
    for q in range(NZ // 4):
        for s in range(4):
            buf[...] = in_ref[4 * q + s].astype(F32)
            off = REST * s
            for xp in range(NX):
                for t in range(2):
                    at = ROWS * (2 * xp + t)
                    row[:ROWS, 128 * t : 128 * t + 128] = buf[at : at + ROWS, :]
                row[:ROWS, 256:384] = buf[8 * ROWS : 9 * ROWS, :]
                rest = row[:, 256:384]
                if xp:
                    rest = pltpu.roll(rest, 128 - REST * xp, 1)
                w = jnp.concatenate([row[:, 0:256], rest], axis=1)
                if off:
                    w = pltpu.roll(w, off, 1)
                at = XSTEP * xp + 1152 * q + 256 * s
                if off:
                    nat[:, at : at + 128] = jnp.where(
                        lane >= off, w[:, 0:128], nat[:, at : at + 128]
                    )
                else:
                    nat[:, at : at + 128] = w[:, 0:128]
                nat[:, at + 128 : at + 384] = w[:, 128:384]
    out_ref[0] = nat[:ROWS, :].astype(BF16)


def first_body(g_ref, m_ref, clip_ref, out_ref, done_ref):
    done_ref[...] = clip_ref[...]
    clip = clip_ref[0:1, 0:1]
    out_ref[0] = (
        beta_first * m_ref[0].astype(F32)
        + (1.0 - beta_first) * clip * g_ref[0].astype(F32)
    ).astype(BF16)


def eliminate_rows(m_ref, first, last):
    sub = lax.broadcasted_iota(jnp.int32, (8, 128), 0)
    lane = lax.broadcasted_iota(jnp.int32, (8, 128), 1)

    def spread(row):
        return jnp.broadcast_to(row, (8, 128))

    def columns(rows, g):
        return [spread(rows[:, 8 * g + c : 8 * g + c + 1]) for c in range(8)]

    cols = columns(m_ref[8 * first : 8 * first + 8, :], first)
    for g in range(first, last):
        at = slice(8 * g, 8 * g + 8)
        here = (lane >= 8 * g) & (lane < 8 * g + 8)
        v = jnp.where(here, jnp.where(lane == 8 * g + sub, 1.0, 0.0), m_ref[at, :])
        if g + 1 < 16:
            w = m_ref[8 * g + 8 : 8 * g + 16, :]
            down, ahead = columns(w, g), columns(w, g + 1)
        scale, pivot, coef = [], [], {}
        for i in range(8):
            rs = lax.rsqrt(spread(cols[i][i : i + 1, :]))
            left = jnp.where(sub > i, cols[i] * rs, 0.0)
            for c in range(i + 1, 8):
                coef[i, c] = spread(left[c : c + 1, :])
                cols[c] = cols[c] - left * coef[i, c]
            if g + 1 < 16:
                k = down[i] * rs
                for c in range(i + 1, 8):
                    down[c] = down[c] - k * coef[i, c]
                for c in range(8):
                    ahead[c] = ahead[c] - k * spread(k[c : c + 1, :])
                down[i] = k
            row = spread(v[i : i + 1, :]) * rs
            v = jnp.where(sub == i, row, v - left * row)
            scale.append(rs)
            pivot.append(row)
        m_ref[at, :] = v
        for r in range(g + 1, 16):
            to = slice(8 * r, 8 * r + 8)
            w = m_ref[to, :]
            if r > g + 1:
                part = columns(w, g)
            w = jnp.where(here, 0.0, w)
            for i in range(8):
                if r > g + 1:
                    k = part[i] * scale[i]
                    for c in range(i + 1, 8):
                        part[c] = part[c] - k * coef[i, c]
                else:
                    k = down[i]
                w = w - k * pivot[i]
            m_ref[to, :] = w
        if g + 1 < 16:
            cols = ahead


def copy_body(in_ref, out_ref):
    out_ref[...] = in_ref[...]


def factor_body(r0, r1, r2, r3, own_ref, out_ref, full, mat, result, diag):
    for d, r in enumerate((r0, r1, r2, r3)):
        unpack_square(r, full.at[XROWS * d : XROWS * (d + 1)])
    rows = full[...]
    across = (((1,), (1,)), ((), ()))

    for c, w in ((0, 256), (256, 256), (512, 128)):
        mat[c:WIDE, c : c + w] = lax.dot_general(
            rows[:, c:],
            rows[:, c : c + w],
            (((0,), (0,)), ((), ())),
            preferred_element_type=F32,
            precision=HIGH,
        )
    r = lax.broadcasted_iota(jnp.int32, (128, 128), 0)
    c = lax.broadcasted_iota(jnp.int32, (128, 128), 1)
    eye, below = r == c, r >= c
    mat[512:WIDE, 512:] = jnp.where(eye & (r >= BK - 512), 1.0, mat[512:WIDE, 512:])
    mat[WIDE:, :] = own_ref[...]

    def panel(p, carry):
        here = pl.ds(pl.multiple_of(128 * p, 128), 128)
        diag[...] = mat[here, here]
        eliminate_rows(diag, 0, 8)

        @pl.when(p < BTILES - 1)
        def _():
            eliminate_rows(diag, 8, 16)

        inv = jnp.where(below, diag[...], 0.0)
        for k in range(BTILES):

            @pl.when(p == k)
            def _(k=k):
                low = 128 * (k + 1)
                part = lax.dot_general(
                    mat[low:, 128 * k : low],
                    inv,
                    across,
                    preferred_element_type=F32,
                    precision=HIGH,
                )
                result[:, 128 * k : low] = part[WIDE - low :]
                for c in range(low, WIDE, 256):
                    w = min(256, WIDE - c)
                    mat[c:, c : c + w] -= lax.dot_general(
                        part[c - low :],
                        part[c - low : c - low + w],
                        across,
                        preferred_element_type=F32,
                        precision=HIGH,
                    )

        return carry

    lax.fori_loop(0, BTILES, panel, 0)
    out_ref[0] = result[:ROWS, :BK]


def local(gradient, first_moment, second_moment, statistic, eigenbasis):
    x = lax.axis_index("x").astype(jnp.int32).reshape(1)

    def swap(v, axis):
        return lax.all_to_all(v, axis, 0, 0, tiled=True)

    def shift(v, axis, d):
        size = lax.axis_size(axis)
        return lax.ppermute(v, axis, [(k, (k + d) % size) for k in range(size)])

    def spread(v, axis="x"):
        return [shift(v, axis, d) if d else v for d in ORDER]

    def deal(parts):
        return [shift(parts[d], "x", d) if d else parts[d] for d in ORDER]

    natural = pltpu.VMEM((16, FF), F32)
    chunk = pltpu.VMEM((PACK, 128), F32)
    rows = pltpu.VMEM((XROWS, PIECES), F32)
    parts = pltpu.VMEM((NX, XROWS, 384), BF16)

    packed, sums = call(
        pack_body,
        [struct((NZ, APACK, 128), BF16), struct((8, 128), F32)],
        [gradient, first_moment],
        [natural, pltpu.VMEM((16, 384), F32), pltpu.VMEM((NZ, APACK, 128), F32)],
    )
    mid = swap(packed, "z")
    sums = spread(sums + shift(sums, "c", 1), "y")
    (b_packed,) = call(
        pack_basis_body,
        struct((NZ, BPACK, 128), F32),
        [eigenbasis],
        [pltpu.VMEM((BPACK, 128), F32)],
        after=sums[1:],
        far=[mid],
    )
    b_mid = swap(b_packed, "z")
    over_x = call(
        unpack_body,
        [struct((XPACK, PIECES), BF16)] * 4,
        [mid, *sums],
        [pltpu.VMEM((APACK, 128), F32), rows, rows, parts],
        at=x,
    )
    share, both = call(
        covariance_body,
        [
            struct((NZ, BPACK, 128), F32),
            struct((NX, XROWS, 768), BF16),
        ],
        deal(over_x),
        [pltpu.VMEM((NX, XROWS, PIECES), BF16), pltpu.VMEM((XROWS, WIDE), F32)],
        at=x,
        flops=2 * XROWS * BK * PIECES,
    )
    share = swap(share, "z")
    basis, rounded = call(
        unpack_basis_body,
        [struct((BK, WIDE), F32), struct((BK, BK), BF16)],
        spread(b_mid),
        [pltpu.VMEM((NX, NZ, BPACK, 128), F32)],
        at=x,
    )

    new_stat, own, r_packed, clip = call(
        refresh_body,
        [
            struct((1, ROWS, BK), F32),
            struct((16, WIDE), F32),
            struct((NZ, BPACK, 128), F32),
            struct((8, 128), F32),
        ],
        [share, statistic, basis],
        [pltpu.VMEM((16, WIDE), F32), pltpu.VMEM((BPACK, 128), F32)],
        flops=12 * 16 * BK * WIDE,
    )
    r_mid = swap(r_packed, "z")

    *up_parts, new_second = call(
        rotate_body,
        [struct((XROWS, 384), BF16)] * 4 + [struct((1, COLS, BK), BF16)],
        [both, rounded, jnp.swapaxes(second_moment, 1, 2), clip],
        [parts],
        at=x,
        flops=6 * BK * BK * 384,
        nbytes=4 << 20,
    )
    up_parts = deal(up_parts)
    new_first, first_done = call(
        first_body,
        [struct((1, ROWS, FF), BF16), struct((8, 128), F32)],
        [gradient, first_moment, clip],
    )
    (r_mid,) = call(
        copy_body,
        struct((NZ, BPACK, 128), F32),
        [r_mid],
        after=[*up_parts[1:], first_done],
    )
    r_parts = spread(r_mid)
    (up_packed,) = call(
        pack_update_body,
        struct((NZ, PACK, 128), BF16),
        up_parts,
        [parts, rows, chunk],
        at=x,
        after=r_parts[1:],
    )
    up_mid = swap(up_packed, "z")

    (new_basis,) = call(
        factor_body,
        struct((1, ROWS, BK), F32),
        [*r_parts, own],
        [
            pltpu.VMEM((BK, WIDE), F32),
            pltpu.VMEM((WIDE + 16, WIDE), F32),
            pltpu.VMEM((16, WIDE), F32),
            pltpu.VMEM((128, 128), F32),
        ],
        flops=12 * BK * WIDE * WIDE,
    )
    (update,) = call(
        unpack_update_body,
        struct((1, ROWS, FF), BF16),
        [up_mid],
        [chunk, pltpu.VMEM((16, 384), F32), natural],
    )
    return update, new_first, jnp.swapaxes(new_second, 1, 2), new_stat, new_basis


def solution(mesh):
    grid = Mesh(mesh.devices.reshape(NX, NZ, 4, 2), ("x", "z", "y", "c"))
    rows = P(("y", "c"), ("x", "z"), None)
    cols = P(("y", "c"), None, ("x", "z"))
    return jax.shard_map(
        local,
        mesh=grid,
        in_specs=(rows, rows, cols, rows, rows),
        out_specs=(rows, rows, cols, rows, rows),
        check_vma=False,
    )
```
